256 devices in a mesh: space: 4 (over z_lo, core), tins: 4 (over y), tsink: 16 (over z_hi, x).
Axes of the slice: x: 4, y: 4, z: 8 (z_hi: 4, z_lo: 2; z = z_hi * 2 + z_lo), core: 2. Of those that a mesh axis runs over, the one named last changes fastest.
Arguments:
- eigvecs: float32 [4, 2, 3, 128, 16, 256], P('tins', None, None, 'tsink', 'space'), may hold values from -0.375 to 0.375
- links: float32 [4, 3, 2, 3, 3, 16, 256], P('tins', None, None, None, None, 'space'), may hold values from -3.5 to 3.5
- momenta: int32 [2, 3], replicated, may hold values from -2 to 2
- directions: int32 [3], replicated, may hold values from 0 to 2
- ins_time: int32 [4], P('tins'), may hold values from 0 to 3, as said below
- sink_time: int32 [16], P('tsink'), may hold values from 1 to 4
- sink_peramb: float32 [16, 4, 2, 512, 512], P('tsink', 'tins', None, 'space'), may hold values from -0.375 to 0.375
- source_peramb: float32 [4, 2, 512, 512], P('tins'), may hold values from -0.1875 to 0.1875
Outputs:
- gen_peramb: float32 [512, 16, 6, 2, 512], P('tins', 'tsink', None, None, 'space')
The draws below stay inside these ranges and needn't reach their ends.
Inputs may be any that keep to these rules, and one draw needn't show every extreme that they name: `ins_time`: each lattice timeslice of the window appears in exactly one slot. `sink_time`: sink timeslices on the numbering of ins_time. `momenta`: momentum components in units of 2 pi / 16. `directions`: 0 is x, 1 is y, 2 is z.
All inputs are finite; a program needn't handle non-finite values.
Results may differ from the reference program's by a relative error of at most 0.0003.
Values sent between devices are 32-bit elements; how exact they have to be, the bound alone decides.
No kernel may reach another device: no remote copies, remote signals or barrier semaphores. Data moves between devices by JAX's collectives and lax.ppermute only.
A program may use at most 64 MiB of HBM per device.

```python
import math
import jax
import jax.numpy as jnp
from jax import lax

L = 16
PLANE = 256
NV = 128
NSPIN = 4
M = 512
NMOM = 2
NDISP = 3
T_INS = 4
T_SINK = 16


def draw_ins_time(key, part):
    return jax.random.permutation(jax.random.fold_in(key, 7), T_INS).astype(jnp.int32)


def touch_ends(array, own_key, least, high):
    place = [jax.random.randint(jax.random.fold_in(own_key, axis), (), 0, length) for axis, length in enumerate(array.shape)]
    longest = array.shape.index(max(array.shape))
    neighbour = place[:longest] + [(place[longest] + 1) % array.shape[longest]] + place[longest + 1:]
    return array.at[tuple(place)].set(least).at[tuple(neighbour)].set(high)


def block_levels(own_key, dims, split, least, top_value):
    loudness = 1.0
    for axis_at, shards_of in split:
        draws = jax.random.uniform(jax.random.fold_in(jax.random.fold_in(own_key, 6), axis_at), (shards_of,), jnp.float32, least / len(split), top_value / len(split))
        loudness = loudness * jnp.repeat(jnp.exp(draws), dims[axis_at] // shards_of).reshape((-1,) + (1,) * (len(dims) - 1 - axis_at))
    return loudness


def scatter_about(key, shape, deviation, limit, split=(), kind=jnp.bfloat16):
    level = block_levels(key, shape, split, -0.22, 0.18) if split else 1.0
    values = jax.random.normal(key, shape, jnp.float32) * deviation * level
    return jnp.minimum(jnp.maximum(values, -limit), limit).astype(kind)


def setup_inputs(seed: int = 0) -> dict:
    arg_keys = jax.random.split(jax.random.key(seed), 9)
    return {
        "eigvecs": scatter_about(arg_keys[0], (T_INS, 2, 3, NV, L, PLANE), (L * L) ** -0.5, 0.375, ((0, 4), (3, 16), (4, 4)), jnp.float32),
        "links": scatter_about(arg_keys[1], (T_INS, 3, 2, 3, 3, L, PLANE), 3 ** -0.5, 3.5, ((0, 4), (5, 4)), jnp.float32),
        "momenta": touch_ends(jax.random.randint(arg_keys[2], (NMOM, 3), -2, 3), jax.random.fold_in(arg_keys[2], 1), -2, 2).astype(jnp.int32),
        "directions": jax.random.randint(arg_keys[3], (NDISP,), 0, 3).astype(jnp.int32),
        "ins_time": draw_ins_time(jax.random.fold_in(arg_keys[8], 71), 0),
        "sink_time": touch_ends(jax.random.randint(arg_keys[5], (T_SINK,), 1, T_INS + 1), jax.random.fold_in(arg_keys[5], 1), 1, T_INS).astype(jnp.int32),
        "sink_peramb": scatter_about(arg_keys[6], (T_SINK, T_INS, 2, M, M), (2 * NV) ** -0.5, 0.375, ((0, 16), (1, 4), (3, 4)), jnp.float32),
        "source_peramb": scatter_about(arg_keys[7], (T_INS, 2, M, M), (2 * M) ** -0.5, 0.1875, ((0, 4),), jnp.float32),
    }


HIGHEST = lax.Precision.HIGHEST


def plane_shift(source, axis_dir, step_sign, side_len):
    if axis_dir == 1:
        return jnp.roll(source, -step_sign * side_len, axis=-1)
    column = lax.broadcasted_iota(jnp.int32, (side_len * side_len,), 0) % side_len
    if step_sign == 1:
        return jnp.where(column == side_len - 1, jnp.roll(source, side_len - 1, axis=-1), jnp.roll(source, -1, axis=-1))
    return jnp.where(column == 0, jnp.roll(source, 1 - side_len, axis=-1), jnp.roll(source, 1, axis=-1))


def color_apply(link_mat, vector, adjoint):
    link_re, link_im = link_mat[:, 0], link_mat[:, 1]
    vec_re, vec_im = vector[:, 0], vector[:, 1]
    rows_real = []
    rows_imag = []
    for colour in range(3):
        sum_real = jnp.zeros_like(vec_re[:, 0])
        sum_imag = jnp.zeros_like(vec_re[:, 0])
        for inner in range(3):
            if adjoint:
                here_re = link_re[:, inner, colour][:, None]
                here_im = -link_im[:, inner, colour][:, None]
            else:
                here_re = link_re[:, colour, inner][:, None]
                here_im = link_im[:, colour, inner][:, None]
            sum_real = sum_real + here_re * vec_re[:, inner] - here_im * vec_im[:, inner]
            sum_imag = sum_imag + here_re * vec_im[:, inner] + here_im * vec_re[:, inner]
        rows_real.append(sum_real)
        rows_imag.append(sum_imag)
    return jnp.stack([jnp.stack(rows_real, axis=1), jnp.stack(rows_imag, axis=1)], axis=1)


def covariant(link_here, link_below, vec_above, vec_below):
    return color_apply(link_here, vec_above, False) - color_apply(link_below, vec_below, True)


def plane_derivs(vectors, link_all, side_len):
    result = []
    for axis_dir in range(2):
        link_here = link_all[:, axis_dir]
        vec_above = plane_shift(vectors, axis_dir, 1, side_len)
        vec_below = plane_shift(vectors, axis_dir, -1, side_len)
        link_below = plane_shift(link_here, axis_dir, -1, side_len)
        result.append(covariant(link_here, link_below, vec_above, vec_below))
    return result


def phase_factors(momenta, z_coord, side_len):
    site_index = lax.broadcasted_iota(jnp.int32, (side_len * side_len,), 0)
    x_coord = site_index % side_len
    y_coord = site_index // side_len
    product = (momenta[:, 0, None, None] * x_coord[None, None, :]
               + momenta[:, 1, None, None] * y_coord[None, None, :]
               + momenta[:, 2, None, None] * z_coord[None, :, None])
    angles = (2.0 * math.pi / side_len) * jnp.mod(product, side_len).astype(jnp.float32)
    return jnp.cos(angles), jnp.sin(angles)


def phase_kets(derivative, directions, momenta, z_coord, side_len):
    onehot = (directions[:, None] == jnp.arange(3, dtype=jnp.int32)[None, :]).astype(jnp.float32)
    chosen = jnp.zeros((derivative.shape[1], onehot.shape[0]) + derivative.shape[2:], jnp.float32)
    for axis_dir in range(3):
        chosen = chosen + onehot[None, :, axis_dir, None, None, None, None, None] * derivative[axis_dir][:, None]
    cos_part, sine_part = phase_factors(momenta, z_coord, side_len)
    cos_part = cos_part[None, :, None, None, None, :, :]
    sine_part = sine_part[None, :, None, None, None, :, :]
    disp_real = chosen[:, None, :, 0]
    disp_imag = chosen[:, None, :, 1]
    wave_real = cos_part * disp_real + sine_part * disp_imag
    wave_imag = cos_part * disp_imag - sine_part * disp_real
    stacked = jnp.concatenate([wave_real, wave_imag], axis=3)
    shape_now = stacked.shape
    return stacked.reshape((shape_now[0], shape_now[1] * shape_now[2]) + shape_now[3:])


def elemental_part(bra_waves, ket_waves, pattern):
    swapped = jnp.concatenate([ket_waves[:, :, 3:], -ket_waves[:, :, :3]], axis=2)
    real_part = jnp.einsum(pattern, bra_waves, ket_waves, precision=HIGHEST)
    imag_part = jnp.einsum(pattern, bra_waves, swapped, precision=HIGHEST)
    return jnp.stack([real_part, imag_part], axis=2)


def left_product(row_block, elemental, weight):
    count_t = row_block.shape[0]
    row_count = row_block.shape[2]
    order_m = row_block.shape[3]
    split_rows = row_block.reshape(count_t, 2, row_count, NSPIN, order_m // NSPIN)
    rows_re, rows_im = split_rows[:, 0], split_rows[:, 1]
    elem_re, elem_im = elemental[:, :, 0], elemental[:, :, 1]

    def contract(first_op, second_op):
        return jnp.einsum("trsa,tqba->tqrsb", first_op, second_op, precision=HIGHEST)

    spin_sign = jnp.where(jnp.arange(NSPIN) < 2, 1.0, -1.0).astype(jnp.float32)
    factor = weight[:, None, None, None, None] * spin_sign[None, None, None, :, None]
    left_re = factor * (contract(rows_re, elem_re) - contract(rows_im, elem_im))
    left_im = factor * (contract(rows_re, elem_im) + contract(rows_im, elem_re))
    pairs = elemental.shape[1]
    return (left_re.reshape(count_t, pairs, row_count, order_m),
            left_im.reshape(count_t, pairs, row_count, order_m))


def right_product(left_re, left_im, src_re, src_im):
    def contract(first_op, second_op):
        return jnp.einsum("tqrk,tkc->cqr", first_op, second_op, precision=HIGHEST)

    gen_re = contract(left_re, src_re) - contract(left_im, src_im)
    gen_im = contract(left_re, src_im) + contract(left_im, src_re)
    return jnp.stack([gen_re, gen_im], axis=2)


def reference(eigvecs, links, momenta, directions, ins_time, sink_time, sink_peramb, source_peramb):
    z_coord = jnp.arange(L, dtype=jnp.int32)

    def one_time(time_pair):
        vector_t = time_pair[0][None]
        link_t = time_pair[1][None]
        derivs = plane_derivs(vector_t, link_t, L)
        link_z = link_t[:, 2]
        derivs.append(covariant(link_z, jnp.roll(link_z, 1, axis=4),
                                jnp.roll(vector_t, -1, axis=4), jnp.roll(vector_t, 1, axis=4)))
        derivative = jnp.stack(derivs)
        ket_waves = phase_kets(derivative, directions, momenta, z_coord, L)
        bra_waves = vector_t.reshape((1, 6) + vector_t.shape[3:])
        return elemental_part(bra_waves, ket_waves, "tkazp,tqkbzp->tqba")[0]

    elemental = lax.map(one_time, (eigvecs, links))
    src_re = source_peramb[:, 0]
    src_im = source_peramb[:, 1]

    def one_sink(sink_pair):
        row_block, sink_limit = sink_pair
        weight = (ins_time < sink_limit).astype(jnp.float32)
        left_re, left_im = left_product(row_block, elemental, weight)
        return right_product(left_re, left_im, src_re, src_im)

    generalized = lax.map(one_sink, (sink_peramb, sink_time))
    return jnp.moveaxis(generalized, 0, 1)
```

```python
import functools
import math

import jax
import jax.numpy as jnp
from jax import lax
from jax.experimental import pallas as pl
from jax.experimental.pallas import tpu as pltpu
from jax.sharding import PartitionSpec as P

L = 16
NSPIN = 4
F32 = jnp.float32
BF16 = jnp.bfloat16
VMEM = pl.BlockSpec(memory_space=pltpu.VMEM)
SMEM = pl.BlockSpec(memory_space=pltpu.SMEM)


def params(mib):
    return pltpu.CompilerParams(vmem_limit_bytes=mib * 2**20)


def halves(value):
    high = value.astype(BF16)
    return high, (value - high.astype(F32)).astype(BF16)


def dot_three(first, second, dims):
    dot = functools.partial(
        lax.dot_general, dimension_numbers=(dims, ((), ())), preferred_element_type=F32
    )
    return dot(first[0], second[0]) + (dot(first[0], second[1]) + dot(first[1], second[0]))


def colour_product(link, vector, adjoint):
    out = []
    for colour in range(3):
        real = imag = None
        for inner in range(3):
            v_re, v_im = vector[inner], vector[3 + inner]
            if adjoint:
                u_re, u_im = link(inner, colour)
                terms = (u_re * v_re + u_im * v_im, u_re * v_im - u_im * v_re)
            else:
                u_re, u_im = link(colour, inner)
                terms = (u_re * v_re - u_im * v_im, u_re * v_im + u_im * v_re)
            real = terms[0] if real is None else real + terms[0]
            imag = terms[1] if imag is None else imag + terms[1]
        out.append((real, imag))
    return [pair[0] for pair in out] + [pair[1] for pair in out]


def shift_x(value, step, column):
    if step == 1:
        return jnp.where(
            column == L - 1, pltpu.roll(value, L - 1, 1), pltpu.roll(value, 127, 1)
        )
    return jnp.where(column == 0, pltpu.roll(value, 128 - L + 1, 1), pltpu.roll(value, 1, 1))


def shift_y(low, high, step, lane):
    if step == 1:
        low, high = pltpu.roll(low, 128 - L, 1), pltpu.roll(high, 128 - L, 1)
        own = lane < 128 - L
    else:
        low, high = pltpu.roll(low, L, 1), pltpu.roll(high, L, 1)
        own = lane >= L
    return jnp.where(own, low, high), jnp.where(own, high, low)


def elemental_kernel(place, *refs):
    bras, kets = refs[0:4], refs[4:8]
    links_xy, links_z, phase, turn, out, waves, phased, total, combined = refs[8:]
    space, z_hi, x_pos = place[0], place[1], place[2]
    lane = lax.broadcasted_iota(jnp.int32, (8, 128), 1)
    column = lane % L
    total[...] = jnp.zeros_like(total)

    def plane(z, carry):
        for block in range(4):
            row = pl.multiple_of(((x_pos + 4 - block) % 4) * 8, 8)
            bra = bras[block]

            def vec(z_at, half):
                lanes = slice(half * 128, half * 128 + 128)
                return [bra[z_at, comp, :, lanes] for comp in range(6)]

            here = [vec(z + 1, half) for half in range(2)]

            def store(axis, sign, values):
                base = (axis * 2 + sign) * 32
                for half in range(2):
                    for comp in range(6):
                        start = comp * 256 + half * 128
                        waves[pl.ds(base + row, 8), start : start + 128] = values[half][comp]

            for axis in range(3):

                def link(ref, z_at, first, half):
                    lanes = slice(half * 128, half * 128 + 128)

                    def get(a, b):
                        real = ref[z_at, first + a * 3 + b : first + a * 3 + b + 1, lanes]
                        imag = ref[z_at, first + 9 + a * 3 + b : first + 10 + a * 3 + b, lanes]
                        return real, imag

                    return get

                if axis < 2:
                    use = [link(links_xy, z, axis * 18, half) for half in range(2)]
                    below = use
                else:
                    use = [link(links_z, z + 1, 0, half) for half in range(2)]
                    below = [link(links_z, z, 0, half) for half in range(2)]
                if axis == 0:
                    above = [[shift_x(v, 1, column) for v in here[h]] for h in range(2)]
                elif axis == 1:
                    pairs = [shift_y(a, b, 1, lane) for a, b in zip(here[0], here[1])]
                    above = [[pair[h] for pair in pairs] for h in range(2)]
                else:
                    above = [vec(z + 2, half) for half in range(2)]
                store(axis, 0, [colour_product(use[h], above[h], False) for h in range(2)])
                source = here if axis < 2 else [vec(z, half) for half in range(2)]
                back = [colour_product(below[h], source[h], True) for h in range(2)]
                if axis == 0:
                    back = [[shift_x(v, -1, column) for v in back[h]] for h in range(2)]
                elif axis == 1:
                    pairs = [shift_y(a, b, -1, lane) for a, b in zip(back[0], back[1])]
                    back = [[pair[h] for pair in pairs] for h in range(2)]
                store(axis, 1, back)

        for block in range(4):
            row = pl.multiple_of(((z_hi + 4 - block) % 4) * 8, 8)
            ket = kets[block]
            for mom in range(2):
                cos = phase[z, mom * 2 : mom * 2 + 1, :]
                sin = phase[z, mom * 2 + 1 : mom * 2 + 2, :]
                for colour in range(3):
                    v_re, v_im = ket[z, colour], ket[z, 3 + colour]
                    w_re = cos * v_re + sin * v_im
                    w_im = cos * v_im - sin * v_re
                    first = slice(colour * 256, colour * 256 + 256)
                    second = slice(768 + colour * 256, 1024 + colour * 256)
                    phased[pl.ds(mom * 64 + row, 8), first] = w_re
                    phased[pl.ds(mom * 64 + row, 8), second] = w_im
                    phased[pl.ds(mom * 64 + 32 + row, 8), first] = w_im
                    phased[pl.ds(mom * 64 + 32 + row, 8), second] = -w_re
        total[...] += dot_three(halves(waves[...]), halves(phased[...]), ((1,), (1,)))
        return carry

    lax.fori_loop(0, 4, plane, 0)

    for block in range(6):
        combined[block] = total[block * 32 : block * 32 + 32, :]
    wide = lax.broadcasted_iota(jnp.int32, (32, 128), 1)
    is_real = wide % 64 < 32
    for pair in range(3):
        axis = place[3 + pair]
        ahead, back = combined[axis * 2], combined[axis * 2 + 1]
        added = ahead + back
        swapped = jnp.where(is_real, pltpu.roll(added, 96, 1), pltpu.roll(added, 32, 1))
        value = turn[0, pair : pair + 1, :] * (back - ahead) + turn[1, pair : pair + 1, :] * swapped
        for group in range(4):
            out[space ^ group, pair] = value[group * 8 : group * 8 + 8, :]


def elemental_blocks(place, bras, kets, links_xy, links_z, phase, turn):
    return pl.pallas_call(
        elemental_kernel,
        out_shape=jax.ShapeDtypeStruct((4, 3, 8, 128), F32),
        in_specs=[SMEM] + [VMEM] * 12,
        out_specs=VMEM,
        scratch_shapes=[
            pltpu.VMEM((192, 1536), F32),
            pltpu.VMEM((128, 1536), F32),
            pltpu.VMEM((192, 128), F32),
            pltpu.VMEM((6, 32, 128), F32),
        ],
        compiler_params=params(24),
        cost_estimate=pl.CostEstimate(flops=10**9, bytes_accessed=3 * 10**6, transcendentals=0),
        name="elementals",
    )(place, *bras, *kets, links_xy, links_z, phase, turn)


def prepare_kernel(weight, source, sink, src_hi, src_lo, sink_hi, sink_lo):
    for part in range(2):
        for spin in range(NSPIN):
            rows = [
                source[part, spin * 128 + i * 32 + j * 8 : spin * 128 + i * 32 + j * 8 + 8, :]
                for j in range(4)
                for i in range(4)
            ]
            turned = jnp.concatenate(rows, axis=0).T
            high, low = halves(turned)
            for block in range(4):
                sign = 1 if part == 0 else -1
                cols = slice(block * 128, block * 128 + 128)
                same = slice(part * 512 + spin * 128, part * 512 + spin * 128 + 128)
                other = slice((1 - part) * 512 + spin * 128, (1 - part) * 512 + spin * 128 + 128)
                src_hi[block, 0:128, same] = sign * high[cols]
                src_lo[block, 0:128, same] = sign * low[cols]
                src_hi[block, 128:256, other] = high[cols]
                src_lo[block, 128:256, other] = low[cols]
    for part in range(2):
        for spin in range(NSPIN):
            sign = 1.0 if spin < 2 else -1.0
            turned = sink[part, :, spin * 128 : spin * 128 + 128].T * (sign * weight[0])
            high, low = halves(turned)
            sink_hi[part * 128 : part * 128 + 128, spin * 128 : spin * 128 + 128] = high
            sink_lo[part * 128 : part * 128 + 128, spin * 128 : spin * 128 + 128] = low


def prepare(weight, source, sink):
    src = jax.ShapeDtypeStruct((4, 256, 1024), BF16)
    snk = jax.ShapeDtypeStruct((256, 512), BF16)
    return pl.pallas_call(
        prepare_kernel,
        out_shape=(src, src, snk, snk),
        in_specs=[SMEM, VMEM, VMEM],
        out_specs=(VMEM,) * 4,
        compiler_params=params(24),
        cost_estimate=pl.CostEstimate(flops=10**8, bytes_accessed=8 * 10**6, transcendentals=0),
        name="prepare",
    )(weight, source, sink)


def left_kernel(elem, sink_hi, sink_lo, left_hi, left_lo):
    for pair in range(3):
        rows_all = []
        for x_pos in range(4):
            tiles = [elem[p, i * 4 + x_pos, pair] for i in range(4) for p in range(4)]
            turned = jnp.concatenate(tiles, axis=0).T
            swapped = jnp.concatenate(
                [-turned[32:64], turned[0:32], -turned[96:128], turned[64:96]], axis=0
            )
            rows_all.append(jnp.concatenate([turned, swapped], axis=1))
        value = dot_three(
            halves(jnp.concatenate(rows_all, axis=0)), (sink_hi[...], sink_lo[...]), ((1,), (0,))
        )
        high, low = halves(value)
        for x_pos in range(4):
            for mom in range(2):
                for part in range(2):
                    start = x_pos * 128 + mom * 64 + part * 32
                    for spin in range(NSPIN):
                        place = part * 512 + spin * 128 + x_pos * 32
                        lanes = slice((mom * 3 + pair) * 128, (mom * 3 + pair) * 128 + 128)
                        cols = slice(spin * 128, spin * 128 + 128)
                        left_hi[place : place + 32, lanes] = high[start : start + 32, cols]
                        left_lo[place : place + 32, lanes] = low[start : start + 32, cols]


def left_product(elem, sink_hi, sink_lo):
    shape = jax.ShapeDtypeStruct((1024, 768), BF16)
    return pl.pallas_call(
        left_kernel,
        out_shape=(shape, shape),
        in_specs=[VMEM] * 3,
        out_specs=(VMEM,) * 2,
        compiler_params=params(24),
        cost_estimate=pl.CostEstimate(flops=10**9, bytes_accessed=4 * 10**6, transcendentals=0),
        name="left",
    )(elem, sink_hi, sink_lo)


def right_kernel(block, src_hi, src_lo, left_hi, left_lo, out_re, out_im):
    value = dot_three(
        (src_hi[0], src_lo[0]), (left_hi[...], left_lo[...]), ((1,), (0,))
    )
    out_re[...] = value[0:128]
    out_im[...] = value[128:256]


def right_product(block, src_hi, src_lo, left_hi, left_lo):
    shape = jax.ShapeDtypeStruct((128, 768), F32)
    spec = pl.BlockSpec((1, 256, 1024), lambda i, ref: (ref[0], 0, 0))
    whole = pl.BlockSpec((1024, 768), lambda i, ref: (0, 0))
    result = pl.BlockSpec((128, 768), lambda i, ref: (0, 0))
    return pl.pallas_call(
        right_kernel,
        out_shape=(shape, shape),
        grid_spec=pltpu.PrefetchScalarGridSpec(
            num_scalar_prefetch=1,
            grid=(1,),
            in_specs=[spec, spec, whole, whole],
            out_specs=(result, result),
        ),
        compiler_params=params(24),
        cost_estimate=pl.CostEstimate(flops=10**9, bytes_accessed=5 * 10**6, transcendentals=0),
        name="right",
    )(block, src_hi, src_lo, left_hi, left_lo)


def final_kernel(*refs):
    out = refs[6]
    for part in range(2):
        value = refs[part][...] + (refs[2 + part][...] + refs[4 + part][...])
        for pair in range(6):
            out[:, pair, part, :] = value[:, pair * 128 : pair * 128 + 128]


def final_sum(*terms):
    return pl.pallas_call(
        final_kernel,
        out_shape=jax.ShapeDtypeStruct((128, 6, 2, 128), F32),
        in_specs=[VMEM] * 6,
        out_specs=VMEM,
        compiler_params=params(16),
        name="final",
    )(*terms)


def ring(count, step):
    return [(i, (i + step) % count) for i in range(count)]


def along_x(step):
    return [(i * 4 + j, i * 4 + (j + step) % 4) for i in range(4) for j in range(4)]


def along_z(step):
    return [(i * 4 + j, ((i + step) % 4) * 4 + j) for i in range(4) for j in range(4)]


def phase_planes(momenta, z_coord):
    site = lax.broadcasted_iota(jnp.int32, (L * L,), 0)
    product = (
        momenta[None, :, 0, None] * (site % L)[None, None, :]
        + momenta[None, :, 1, None] * (site // L)[None, None, :]
        + momenta[None, :, 2, None] * z_coord[:, None, None]
    )
    angles = 2.0 * math.pi / L * jnp.mod(product, L).astype(F32)
    return jnp.stack([jnp.cos(angles), jnp.sin(angles)], axis=2).reshape(-1, 4, L * L)


def step_phases(momenta, directions):
    steps = jnp.stack([momenta[:, directions[e]] for e in range(3)], axis=0)
    angles = 2.0 * math.pi / L * jnp.mod(steps, L).astype(F32)
    cos, sin = jnp.cos(angles), jnp.sin(angles)
    cos = jnp.broadcast_to(cos[:, :, None, None], (3, 2, 2, 32))
    signs = jnp.array([-1.0, 1.0], F32)[None, None, :, None]
    sin = jnp.broadcast_to(sin[:, :, None, None] * signs, (3, 2, 2, 32))
    return jnp.stack([cos.reshape(3, 128), sin.reshape(3, 128)])


def on_device(eigvecs, links, momenta, directions, ins_time, sink_time, sink_peramb, source_peramb):
    depth = eigvecs.shape[4]
    space, tins, tsink = (lax.axis_index(name) for name in ("space", "tins", "tsink"))

    own = jnp.transpose(eigvecs[0].reshape(6, 8, depth, 256), (2, 0, 1, 3))
    planes = jnp.transpose(links[0].reshape(3, 18, depth, 256), (2, 0, 1, 3))
    links_xy = planes[:, :2].reshape(depth, 36, 256)
    top = jnp.concatenate([own[depth - 1].reshape(48, 256), planes[depth - 1, 2]], axis=0)
    top = lax.ppermute(top, "space", ring(4, 1))
    above = lax.ppermute(own[0], "space", ring(4, -1))
    links_z = jnp.concatenate([top[None, 48:], planes[:, 2]], axis=0)
    kets = [own] + [lax.ppermute(own, "tsink", along_z(step)) for step in (1, 2, 3)]
    bra = jnp.concatenate([top[None, :48].reshape(1, 6, 8, 256), own, above[None]], axis=0)
    bras = [bra] + [lax.ppermute(bra, "tsink", along_x(step)) for step in (1, 2, 3)]

    weight = (ins_time < sink_time[0]).astype(F32)
    src_hi, src_lo, sink_hi, sink_lo = prepare(weight, source_peramb[0], sink_peramb[0, 0])

    phase = phase_planes(momenta, space * depth + jnp.arange(depth, dtype=jnp.int32))
    turn = step_phases(momenta, directions)
    place = jnp.concatenate(
        [jnp.stack([space, tsink // 4, tsink % 4]).astype(jnp.int32), directions]
    )
    blocks = elemental_blocks(place, bras, kets, links_xy, links_z, phase, turn)
    summed = blocks[0]
    for other in (2, 3, 1):
        summed = summed + lax.ppermute(blocks[other], "space", [(i, i ^ other) for i in range(4)])
    copies = jnp.broadcast_to(summed[None], (16,) + summed.shape)
    group = lax.all_to_all(copies, "tsink", 0, 0, tiled=True)
    elem = lax.all_gather(group, "space", axis=0, tiled=False)

    left_hi, left_lo = left_product(elem, sink_hi, sink_lo)

    def right(offset):
        block = ((tins + offset) % 4).astype(jnp.int32)[None]
        return right_product(block, src_hi, src_lo, left_hi, left_lo)

    def up(value):
        return lax.ppermute(value, "tins", ring(4, 1))

    def down(value):
        return lax.ppermute(value, "tins", ring(4, -1))

    far_re, far_im = right(2)
    from_below, from_above = up(far_re), down(far_im)
    next_re, next_im = right(1)
    below_im = up(next_im)
    prev_re, prev_im = right(3)
    above_re = down(prev_re)
    own_re, own_im = right(0)
    below_re = up(next_re + from_below)
    above_im = down(prev_im + from_above)
    return final_sum(own_re, own_im, below_re, below_im, above_re, above_im)[:, None]


def solution(mesh):
    in_specs = (
        P("tins", None, None, "tsink", "space", None),
        P("tins", None, None, None, None, "space", None),
        P(),
        P(),
        P("tins"),
        P("tsink"),
        P("tsink", "tins", None, "space", None),
        P("tins", None, None, None),
    )
    out_specs = P("tins", "tsink", None, None, "space")
    return jax.shard_map(
        on_device, mesh=mesh, in_specs=in_specs, out_specs=out_specs, check_vma=False
    )
```

```python
import functools
import math

import jax
import jax.numpy as jnp
from jax import lax
from jax.experimental import pallas as pl
from jax.experimental.pallas import tpu as pltpu
from jax.sharding import PartitionSpec as P

L = 16
NSPIN = 4
F32 = jnp.float32
BF16 = jnp.bfloat16
VMEM = pl.BlockSpec(memory_space=pltpu.VMEM)
SMEM = pl.BlockSpec(memory_space=pltpu.SMEM)


def params(mib):
    return pltpu.CompilerParams(vmem_limit_bytes=mib * 2**20)


def halves(value):
    high = value.astype(BF16)
    return high, (value - high.astype(F32)).astype(BF16)


def dot_three(first, second, dims):
    dot = functools.partial(
        lax.dot_general, dimension_numbers=(dims, ((), ())), preferred_element_type=F32
    )
    return dot(first[0], second[0]) + (dot(first[0], second[1]) + dot(first[1], second[0]))


def colour_product(link, vector, adjoint):
    out = []
    for colour in range(3):
        real = imag = None
        for inner in range(3):
            v_re, v_im = vector[inner], vector[3 + inner]
            if adjoint:
                u_re, u_im = link(inner, colour)
                terms = (u_re * v_re + u_im * v_im, u_re * v_im - u_im * v_re)
            else:
                u_re, u_im = link(colour, inner)
                terms = (u_re * v_re - u_im * v_im, u_re * v_im + u_im * v_re)
            real = terms[0] if real is None else real + terms[0]
            imag = terms[1] if imag is None else imag + terms[1]
        out.append((real, imag))
    return [pair[0] for pair in out] + [pair[1] for pair in out]


def shift_x(value, step, column):
    if step == 1:
        return jnp.where(
            column == L - 1, pltpu.roll(value, L - 1, 1), pltpu.roll(value, 127, 1)
        )
    return jnp.where(column == 0, pltpu.roll(value, 128 - L + 1, 1), pltpu.roll(value, 1, 1))


def shift_y(low, high, step, lane):
    if step == 1:
        low, high = pltpu.roll(low, 128 - L, 1), pltpu.roll(high, 128 - L, 1)
        own = lane < 128 - L
    else:
        low, high = pltpu.roll(low, L, 1), pltpu.roll(high, L, 1)
        own = lane >= L
    return jnp.where(own, low, high), jnp.where(own, high, low)


def z_place():
    return lax.shift_right_logical(lax.axis_index("tsink").astype(jnp.int32), 2)


def x_place():
    return lax.axis_index("tsink").astype(jnp.int32) & 3


def block_readers(refs):
    def whole(ref):
        return lambda z, comp, lanes: ref[comp // 3, z, comp % 3, :, lanes]

    def pair(real, imag):
        return lambda z, comp, lanes: (real, imag)[comp // 3][z, comp % 3, :, lanes]

    return [whole(refs[0]), whole(refs[1]), pair(refs[2], refs[3]), whole(refs[4])]


def elemental_kernel(directions, *refs):
    bras, kets = block_readers(refs[0:5]), block_readers(refs[5:10])
    links, low_links, phase, turn, out, waves, phased, total, combined = refs[10:]
    space, z_hi, x_pos = lax.axis_index("space"), z_place(), x_place()
    lane = lax.broadcasted_iota(jnp.int32, (8, 128), 1)
    column = lane % L
    total[...] = jnp.zeros_like(total)

    for z in range(4):
        for block in range(4):
            row = pl.multiple_of(((x_pos + 4 - block) % 4) * 8, 8)
            bra = bras[block]

            def vec(z_at, half):
                lanes = slice(half * 128, half * 128 + 128)
                return [bra(z_at, comp, lanes) for comp in range(6)]

            here = [vec(z + 1, half) for half in range(2)]

            def store(axis, sign, values):
                base = (axis * 2 + sign) * 32
                for half in range(2):
                    for comp in range(6):
                        start = comp * 256 + half * 128
                        waves[pl.ds(base + row, 8), start : start + 128] = values[half][comp]

            for axis in range(3):

                def link(half, shifted):
                    lanes = slice(half * 128, half * 128 + 128)

                    def row(index):
                        if not shifted:
                            return links[axis * 18 + index, z : z + 1, lanes]
                        if z == 0:
                            return low_links[48 + index : 49 + index, lanes]
                        return links[axis * 18 + index, z - 1 : z, lanes]

                    return lambda a, b: (row(a * 3 + b), row(9 + a * 3 + b))

                use = [link(half, False) for half in range(2)]
                below = [link(half, axis == 2) for half in range(2)]
                if axis == 0:
                    above = [[shift_x(v, 1, column) for v in here[h]] for h in range(2)]
                elif axis == 1:
                    pairs = [shift_y(a, b, 1, lane) for a, b in zip(here[0], here[1])]
                    above = [[pair[h] for pair in pairs] for h in range(2)]
                else:
                    above = [vec(z + 2, half) for half in range(2)]
                store(axis, 0, [colour_product(use[h], above[h], False) for h in range(2)])
                source = here if axis < 2 else [vec(z, half) for half in range(2)]
                back = [colour_product(below[h], source[h], True) for h in range(2)]
                if axis == 0:
                    back = [[shift_x(v, -1, column) for v in back[h]] for h in range(2)]
                elif axis == 1:
                    pairs = [shift_y(a, b, -1, lane) for a, b in zip(back[0], back[1])]
                    back = [[pair[h] for pair in pairs] for h in range(2)]
                store(axis, 1, back)

        for block in range(4):
            row = pl.multiple_of(((z_hi + 4 - block) % 4) * 8, 8)
            ket = kets[block]
            for mom in range(2):
                cos = phase[mom * 2, z : z + 1, :]
                sin = phase[mom * 2 + 1, z : z + 1, :]
                for colour in range(3):
                    v_re, v_im = ket(z, colour, slice(0, 256)), ket(z, 3 + colour, slice(0, 256))
                    w_re = cos * v_re + sin * v_im
                    w_im = cos * v_im - sin * v_re
                    first = slice(colour * 256, colour * 256 + 256)
                    second = slice(768 + colour * 256, 1024 + colour * 256)
                    phased[pl.ds(mom * 64 + row, 8), first] = w_re
                    phased[pl.ds(mom * 64 + row, 8), second] = w_im
                    phased[pl.ds(mom * 64 + 32 + row, 8), first] = w_im
                    phased[pl.ds(mom * 64 + 32 + row, 8), second] = -w_re
        total[...] += dot_three(halves(waves[...]), halves(phased[...]), ((1,), (1,)))

    for block in range(6):
        combined[block] = total[block * 32 : block * 32 + 32, :]
    wide = lax.broadcasted_iota(jnp.int32, (32, 128), 1)
    is_real = wide % 64 < 32
    for pair in range(3):
        axis = directions[pair]
        ahead, back = combined[axis * 2], combined[axis * 2 + 1]
        added = ahead + back
        swapped = jnp.where(is_real, pltpu.roll(added, 96, 1), pltpu.roll(added, 32, 1))
        value = turn[0, pair, 0:1] * (back - ahead) + turn[1, pair, 0:1] * swapped
        for group in range(4):
            out[(space % 2) ^ (group % 2), group // 2, pair] = value[group * 8 : group * 8 + 8, :]


def elemental_blocks(directions, bras, kets, links, low_links, phase, turn):
    return pl.pallas_call(
        elemental_kernel,
        out_shape=jax.ShapeDtypeStruct((2, 2, 3, 8, 128), F32),
        in_specs=[SMEM] + [VMEM] * 14,
        out_specs=VMEM,
        scratch_shapes=[
            pltpu.VMEM((192, 1536), F32),
            pltpu.VMEM((128, 1536), F32),
            pltpu.VMEM((192, 128), F32),
            pltpu.VMEM((6, 32, 128), F32),
        ],
        compiler_params=params(24),
        cost_estimate=pl.CostEstimate(flops=10**9, bytes_accessed=3 * 10**6, transcendentals=0),
        name="elementals",
    )(directions, *bras, *kets, links, low_links, phase, turn)


def prepare_kernel(ins_time, sink_time, momenta, directions, source, sink, far_hi, far_lo, near_hi,
                   near_lo, own_hi, own_lo, sink_hi, sink_lo, phase, turn, turned):
    tins = lax.axis_index("tins").astype(jnp.int32)
    weight = jnp.where(ins_time[0] < sink_time[0], 1.0, 0.0)
    site = lax.broadcasted_iota(jnp.int32, (4, L * L), 1)
    z_at = lax.axis_index("space").astype(jnp.int32) * 4 + lax.broadcasted_iota(jnp.int32, (4, L * L), 0)
    for mom in range(2):
        product = momenta[mom, 0] * (site & 15) + momenta[mom, 1] * (site >> 4) + momenta[mom, 2] * z_at
        angles = 2.0 * math.pi / L * (product & 15).astype(F32)
        phase[2 * mom] = jnp.cos(angles)
        phase[2 * mom + 1] = jnp.sin(angles)
    lane = lax.broadcasted_iota(jnp.int32, (8, 128), 1)
    for pair in range(3):
        axis = directions[pair]
        step = jnp.where(lane < 64, momenta[0, axis], momenta[1, axis])
        angles = 2.0 * math.pi / L * (step & 15).astype(F32)
        turn[0, pair] = jnp.cos(angles)
        turn[1, pair] = jnp.where(lane % 64 < 32, -jnp.sin(angles), jnp.sin(angles))
    slots = (
        (2, far_hi, far_lo, 0),
        (1, near_hi, near_lo, 0),
        (3, near_hi, near_lo, 256),
        (0, own_hi, own_lo, 0),
    )
    for part in range(2):
        for spin in range(NSPIN):
            rows = [
                source[part, spin * 128 + i * 32 + j * 8 : spin * 128 + i * 32 + j * 8 + 8, :]
                for j in range(4)
                for i in range(4)
            ]
            turned[...] = jnp.concatenate(rows, axis=0).T
            sign = 1 if part == 0 else -1
            same = slice(part * 512 + spin * 128, part * 512 + spin * 128 + 128)
            other = slice((1 - part) * 512 + spin * 128, (1 - part) * 512 + spin * 128 + 128)
            for offset, to_hi, to_lo, top in slots:
                block = pl.multiple_of(((tins + offset) & 3) * 128, 128)
                high, low = halves(turned[pl.ds(block, 128), :])
                to_hi[top : top + 128, same] = sign * high
                to_lo[top : top + 128, same] = sign * low
                to_hi[top + 128 : top + 256, other] = high
                to_lo[top + 128 : top + 256, other] = low
    for part in range(2):
        for spin in range(NSPIN):
            sign = 1.0 if spin < 2 else -1.0
            value = sink[part, :, spin * 128 : spin * 128 + 128].T * (sign * weight)
            high, low = halves(value)
            sink_hi[part * 128 : part * 128 + 128, spin * 128 : spin * 128 + 128] = high
            sink_lo[part * 128 : part * 128 + 128, spin * 128 : spin * 128 + 128] = low


def prepare(ins_time, sink_time, momenta, directions, source, sink):
    one = jax.ShapeDtypeStruct((256, 1024), BF16)
    two = jax.ShapeDtypeStruct((512, 1024), BF16)
    snk = jax.ShapeDtypeStruct((256, 512), BF16)
    phases = (
        jax.ShapeDtypeStruct((4, 4, 256), F32),
        jax.ShapeDtypeStruct((2, 3, 8, 128), F32),
    )
    return pl.pallas_call(
        prepare_kernel,
        out_shape=(one, one, two, two, one, one, snk, snk) + phases,
        in_specs=[SMEM] * 4 + [VMEM] * 2,
        out_specs=(VMEM,) * 10,
        scratch_shapes=[pltpu.VMEM((512, 128), F32)],
        compiler_params=params(12),
        cost_estimate=pl.CostEstimate(flops=10**8, bytes_accessed=8 * 10**6, transcendentals=0),
        name="prepare",
    )(ins_time, sink_time, momenta, directions, source, sink)


def left_kernel(mine, others, sink_hi, sink_lo, src_hi, src_lo, left_hi, left_lo, out_re, out_im):
    core, z_hi, x_at = lax.axis_index("space") & 1, z_place(), x_place()
    for pair in range(3):
        rows_all = []
        for x_pos in range(4):
            from_x = (x_at - x_pos) & 3
            tiles = []
            for i in range(4):
                from_z = (z_hi - i) & 3
                for group in range(2):
                    own = mine[from_x, from_z, group, pair]
                    other = others[from_x, from_z, group, pair]
                    tiles.append(jnp.where(core == 0, own, other))
                    tiles.append(jnp.where(core == 0, other, own))
            turned = jnp.concatenate(tiles, axis=0).T
            swapped = jnp.concatenate(
                [-turned[32:64], turned[0:32], -turned[96:128], turned[64:96]], axis=0
            )
            rows_all.append(jnp.concatenate([turned, swapped], axis=1))
        value = dot_three(
            halves(jnp.concatenate(rows_all, axis=0)), (sink_hi[...], sink_lo[...]), ((1,), (0,))
        )
        high, low = halves(value)
        for x_pos in range(4):
            for mom in range(2):
                for part in range(2):
                    start = x_pos * 128 + mom * 64 + part * 32
                    for spin in range(NSPIN):
                        at = part * 512 + spin * 128 + x_pos * 32
                        lanes = slice((mom * 3 + pair) * 128, (mom * 3 + pair) * 128 + 128)
                        cols = slice(spin * 128, spin * 128 + 128)
                        left_hi[at : at + 32, lanes] = high[start : start + 32, cols]
                        left_lo[at : at + 32, lanes] = low[start : start + 32, cols]
    right_kernel(src_hi, src_lo, left_hi, left_lo, out_re, out_im)


def left_product(mine, others, sink_hi, sink_lo, src_hi, src_lo):
    shape = jax.ShapeDtypeStruct((1024, 768), BF16)
    result = jax.ShapeDtypeStruct((128, 768), F32)
    return pl.pallas_call(
        left_kernel,
        out_shape=(shape, shape, result, result),
        in_specs=[VMEM] * 6,
        out_specs=(VMEM,) * 4,
        compiler_params=params(16),
        cost_estimate=pl.CostEstimate(flops=10**9, bytes_accessed=4 * 10**6, transcendentals=0),
        name="left",
    )(mine, others, sink_hi, sink_lo, src_hi, src_lo)


def right_kernel(src_hi, src_lo, left_hi, left_lo, *outs):
    for block in range(len(outs) // 2):
        rows = slice(block * 256, block * 256 + 256)
        value = dot_three(
            (src_hi[rows, :], src_lo[rows, :]), (left_hi[...], left_lo[...]), ((1,), (0,))
        )
        outs[2 * block][...] = value[0:128]
        outs[2 * block + 1][...] = value[128:256]


def right_product(src_hi, src_lo, left_hi, left_lo):
    count = 2 * (src_hi.shape[0] // 256)
    return pl.pallas_call(
        right_kernel,
        out_shape=(jax.ShapeDtypeStruct((128, 768), F32),) * count,
        in_specs=[VMEM] * 4,
        out_specs=(VMEM,) * count,
        compiler_params=params(16),
        cost_estimate=pl.CostEstimate(flops=10**9, bytes_accessed=5 * 10**6, transcendentals=0),
        name="right",
    )(src_hi, src_lo, left_hi, left_lo)


def relay_kernel(first, second, third, fourth, out_one, out_two):
    out_one[...] = first[...] + second[...]
    out_two[...] = third[...] + fourth[...]


def relay_sums(*terms):
    shape = jax.ShapeDtypeStruct((128, 768), F32)
    return pl.pallas_call(
        relay_kernel,
        out_shape=(shape, shape),
        in_specs=[VMEM] * 4,
        out_specs=(VMEM,) * 2,
        compiler_params=params(8),
        name="relay",
    )(*terms)


def final_kernel(*refs):
    out = refs[6]
    for part in range(2):
        value = refs[part][...] + (refs[2 + part][...] + refs[4 + part][...])
        for pair in range(6):
            out[:, pair, part, :] = value[:, pair * 128 : pair * 128 + 128]


def final_sum(*terms):
    return pl.pallas_call(
        final_kernel,
        out_shape=jax.ShapeDtypeStruct((128, 6, 2, 128), F32),
        in_specs=[VMEM] * 6,
        out_specs=VMEM,
        compiler_params=params(8),
        name="final",
    )(*terms)


def ring(count, step):
    return [(i, (i + step) % count) for i in range(count)]


def along_x(step):
    return [(i * 4 + j, i * 4 + (j + step) % 4) for i in range(4) for j in range(4)]


def along_z(step):
    return [(i * 4 + j, ((i + step) % 4) * 4 + j) for i in range(4) for j in range(4)]


def gathered(block, along):
    behind = lax.ppermute(block, "tsink", along(1))
    ahead = lax.ppermute(block, "tsink", along(-1))
    real = lax.ppermute(behind[0], "tsink", along(1))
    imag = lax.ppermute(ahead[1], "tsink", along(-1))
    return [block, behind, real, imag, ahead]


def on_device(eigvecs, links, momenta, directions, ins_time, sink_time, sink_peramb, source_peramb):
    depth = eigvecs.shape[4]
    own = lax.optimization_barrier(jnp.transpose(eigvecs[0], (0, 3, 1, 2, 4)))
    links = links[0].reshape(54, depth, 256)
    top = jnp.concatenate([own[:, depth - 1].reshape(48, 256), links[36:, depth - 1]], axis=0)
    top = lax.ppermute(top, "space", ring(4, 1))
    above = lax.ppermute(own[:, 0], "space", ring(4, -1))
    kets = gathered(own, along_z)
    below = top[:48].reshape(2, 1, 3, 8, 256)
    bras = gathered(jnp.concatenate([below, own, above[:, None]], axis=1), along_x)

    sources = prepare(
        ins_time, sink_time, momenta, directions, source_peramb[0], sink_peramb[0, 0]
    )
    far_hi, far_lo, near_hi, near_lo, own_hi, own_lo, sink_hi, sink_lo, phase, turn = sources

    blocks = elemental_blocks(directions, bras, kets, links, top, phase, turn)
    core_pairs = [(i, i ^ 1) for i in range(4)]
    chip_pairs = [(i, i ^ 2) for i in range(4)]
    summed = blocks[0] + lax.ppermute(blocks[1], "space", core_pairs)
    summed = summed + lax.ppermute(summed, "space", chip_pairs)
    for along in (along_z, along_x):
        summed = jnp.stack([summed] + [lax.ppermute(summed, "tsink", along(d)) for d in (1, 2, 3)])
    others = lax.ppermute(summed, "space", core_pairs)

    left_hi, left_lo, far_re, far_im = left_product(
        summed, others, sink_hi, sink_lo, far_hi, far_lo
    )

    def up(value):
        return lax.ppermute(value, "tins", ring(4, 1))

    def down(value):
        return lax.ppermute(value, "tins", ring(4, -1))

    from_below, from_above = up(far_re), down(far_im)
    next_re, next_im, prev_re, prev_im = right_product(near_hi, near_lo, left_hi, left_lo)
    below_im, above_re = up(next_im), down(prev_re)
    own_re, own_im = right_product(own_hi, own_lo, left_hi, left_lo)
    next_re, prev_im = relay_sums(next_re, from_below, prev_im, from_above)
    below_re, above_im = up(next_re), down(prev_im)
    return final_sum(own_re, own_im, below_re, below_im, above_re, above_im)[:, None]


def solution(mesh):
    in_specs = (
        P("tins", None, None, "tsink", "space", None),
        P("tins", None, None, None, None, "space", None),
        P(),
        P(),
        P("tins"),
        P("tsink"),
        P("tsink", "tins", None, "space", None),
        P("tins", None, None, None),
    )
    out_specs = P("tins", "tsink", None, None, "space")
    return jax.shard_map(
        on_device, mesh=mesh, in_specs=in_specs, out_specs=out_specs, check_vma=False
    )
```

```python
import functools
import math

import jax
import jax.numpy as jnp
from jax import lax
from jax.experimental import pallas as pl
from jax.experimental.pallas import tpu as pltpu
from jax.sharding import PartitionSpec as P

L = 16
NSPIN = 4
F32 = jnp.float32
BF16 = jnp.bfloat16
VMEM = pl.BlockSpec(memory_space=pltpu.VMEM)
SMEM = pl.BlockSpec(memory_space=pltpu.SMEM)


def params(mib):
    return pltpu.CompilerParams(vmem_limit_bytes=mib * 2**20)


def halves(value):
    high = value.astype(BF16)
    return high, (value - high.astype(F32)).astype(BF16)


def dot_three(first, second, dims):
    dot = functools.partial(
        lax.dot_general, dimension_numbers=(dims, ((), ())), preferred_element_type=F32
    )
    return dot(first[0], second[0]) + (dot(first[0], second[1]) + dot(first[1], second[0]))


def colour_product(link, vector, adjoint):
    out = []
    for colour in range(3):
        real = imag = None
        for inner in range(3):
            v_re, v_im = vector[inner], vector[3 + inner]
            if adjoint:
                u_re, u_im = link(inner, colour)
                terms = (u_re * v_re + u_im * v_im, u_re * v_im - u_im * v_re)
            else:
                u_re, u_im = link(colour, inner)
                terms = (u_re * v_re - u_im * v_im, u_re * v_im + u_im * v_re)
            real = terms[0] if real is None else real + terms[0]
            imag = terms[1] if imag is None else imag + terms[1]
        out.append((real, imag))
    return [pair[0] for pair in out] + [pair[1] for pair in out]


def shift_x(value, step, column):
    if step == 1:
        return jnp.where(
            column == L - 1, pltpu.roll(value, L - 1, 1), pltpu.roll(value, 127, 1)
        )
    return jnp.where(column == 0, pltpu.roll(value, 128 - L + 1, 1), pltpu.roll(value, 1, 1))


def shift_y(low, high, step, lane):
    if step == 1:
        low, high = pltpu.roll(low, 128 - L, 1), pltpu.roll(high, 128 - L, 1)
        own = lane < 128 - L
    else:
        low, high = pltpu.roll(low, L, 1), pltpu.roll(high, L, 1)
        own = lane >= L
    return jnp.where(own, low, high), jnp.where(own, high, low)


def z_place():
    return lax.shift_right_logical(lax.axis_index("tsink").astype(jnp.int32), 2)


def x_place():
    return lax.axis_index("tsink").astype(jnp.int32) & 3


def block_readers(refs):
    def whole(ref):
        return lambda z, comp, lanes: ref[comp // 3, z, comp % 3, :, lanes]

    def pair(real, imag):
        return lambda z, comp, lanes: (real, imag)[comp // 3][z, comp % 3, :, lanes]

    readers, at = [], 0
    while at < len(refs):
        if len(refs[at].shape) == 5:
            readers.append(whole(refs[at]))
            at += 1
        else:
            readers.append(pair(refs[at], refs[at + 1]))
            at += 2
    return readers


def pack_kernel(eig_far, own, eig, sem):
    copy = pltpu.make_async_copy(eig_far, eig, sem)
    copy.start()
    copy.wait()
    for part in range(2):
        for colour in range(3):
            for z in range(4):
                own[part, z, colour] = eig[part, colour, :, z, :]


def packed(eig):
    return pl.pallas_call(
        pack_kernel,
        out_shape=jax.ShapeDtypeStruct((2, 4, 3, 8, 256), F32),
        in_specs=[pl.BlockSpec(memory_space=pltpu.HBM)],
        out_specs=VMEM,
        scratch_shapes=[pltpu.VMEM((2, 3, 8, 4, 256), F32), pltpu.SemaphoreType.DMA],
        compiler_params=params(8),
        name="pack",
    )(eig)


def waves_kernel(count, *refs):
    blocks = block_readers(refs[: len(refs) - 2 - 2 * count])
    links, low_links = refs[len(refs) - 2 - 2 * count : len(refs) - 2 * count]
    outs = refs[len(refs) - 2 * count :]
    lane = lax.broadcasted_iota(jnp.int32, (8, 128), 1)
    column = lane % L
    for z in range(4):
        for block, read in enumerate(blocks):
            high, low = outs[2 * block], outs[2 * block + 1]

            def vec(z_at, half):
                lanes = slice(half * 128, half * 128 + 128)
                return [read(z_at, comp, lanes) for comp in range(6)]

            here = [vec(z + 1, half) for half in range(2)]
            for axis in range(3):

                def link(half, shifted):
                    lanes = slice(half * 128, half * 128 + 128)

                    def row(index):
                        if not shifted:
                            return links[axis * 18 + index, z : z + 1, lanes]
                        if z == 0:
                            return low_links[index : index + 1, lanes]
                        return links[axis * 18 + index, z - 1 : z, lanes]

                    return lambda a, b: (row(a * 3 + b), row(9 + a * 3 + b))

                use = [link(half, False) for half in range(2)]
                below = [link(half, axis == 2) for half in range(2)]
                if axis == 0:
                    above = [[shift_x(v, 1, column) for v in here[h]] for h in range(2)]
                elif axis == 1:
                    pairs = [shift_y(a, b, 1, lane) for a, b in zip(here[0], here[1])]
                    above = [[pair[h] for pair in pairs] for h in range(2)]
                else:
                    above = [vec(z + 2, half) for half in range(2)]
                ahead = [colour_product(use[h], above[h], False) for h in range(2)]
                source = here if axis < 2 else [vec(z, half) for half in range(2)]
                back = [colour_product(below[h], source[h], True) for h in range(2)]
                if axis == 0:
                    back = [[shift_x(v, -1, column) for v in back[h]] for h in range(2)]
                elif axis == 1:
                    pairs = [shift_y(a, b, -1, lane) for a, b in zip(back[0], back[1])]
                    back = [[pair[h] for pair in pairs] for h in range(2)]
                for half in range(2):
                    for comp in range(6):
                        cols = slice(comp * 256 + half * 128, comp * 256 + half * 128 + 128)
                        both = jnp.concatenate([ahead[half][comp], back[half][comp]], axis=0)
                        parts = halves(both)
                        high[z, axis * 16 : axis * 16 + 16, cols] = parts[0]
                        low[z, axis * 16 : axis * 16 + 16, cols] = parts[1]


def wave_blocks(count, blocks, links, low_links):
    shape = jax.ShapeDtypeStruct((4, 48, 1536), BF16)
    return pl.pallas_call(
        functools.partial(waves_kernel, count),
        out_shape=(shape,) * (2 * count),
        in_specs=[VMEM] * (len(blocks) + 2),
        out_specs=(VMEM,) * (2 * count),
        compiler_params=params(8),
        cost_estimate=pl.CostEstimate(
            flops=count * 10**7, bytes_accessed=count * 2 * 10**6, transcendentals=0
        ),
        name="waves",
    )(*blocks, links, low_links)


def elemental_kernel(directions, *refs):
    kets = block_readers(refs[0:5])
    waves = refs[5:13]
    phase, turn, out, phased, total = refs[13:]
    core, z_hi, x_at = lax.axis_index("space").astype(jnp.int32) & 1, z_place(), x_place()
    for z in range(4):
        for block in range(4):
            row = pl.multiple_of(((z_hi - block) & 3) * 8, 8)
            ket = kets[block]
            for mom in range(2):
                cos = phase[mom * 2, z : z + 1, :]
                sin = phase[mom * 2 + 1, z : z + 1, :]
                for colour in range(3):
                    v_re, v_im = ket(z, colour, slice(0, 256)), ket(z, 3 + colour, slice(0, 256))
                    w_re = cos * v_re + sin * v_im
                    w_im = cos * v_im - sin * v_re
                    first = slice(colour * 256, colour * 256 + 256)
                    second = slice(768 + colour * 256, 1024 + colour * 256)
                    phased[pl.ds(mom * 64 + row, 8), first] = w_re
                    phased[pl.ds(mom * 64 + row, 8), second] = w_im
                    phased[pl.ds(mom * 64 + 32 + row, 8), first] = w_im
                    phased[pl.ds(mom * 64 + 32 + row, 8), second] = -w_re
        bras = jnp.concatenate(
            [waves[2 * block + part][z] for part in range(2) for block in range(4)], axis=0
        )
        value = lax.dot_general(
            bras,
            jnp.concatenate(halves(phased[...]), axis=0),
            (((1,), (1,)), ((), ())),
            preferred_element_type=F32,
        )
        value = value[:192] + value[192:]
        value = value[:, :128] + value[:, 128:]
        total[...] = value if z == 0 else total[...] + value

    is_real = lax.broadcasted_iota(jnp.int32, (8, 128), 1) % 64 < 32
    for pair in range(3):
        axis = directions[pair]
        for block in range(4):
            row = pl.multiple_of(block * 48 + axis * 16, 16)
            ahead, back = total[pl.ds(row, 8), :], total[pl.ds(row + 8, 8), :]
            added = ahead + back
            swapped = jnp.where(is_real, pltpu.roll(added, 96, 1), pltpu.roll(added, 32, 1))
            group = (x_at - block) & 3
            out[core ^ (group & 1), lax.shift_right_logical(group, 1), pair] = (
                turn[0, pair] * (back - ahead) + turn[1, pair] * swapped
            )


def elemental_blocks(directions, kets, waves, phase, turn):
    return pl.pallas_call(
        elemental_kernel,
        out_shape=jax.ShapeDtypeStruct((2, 2, 3, 8, 128), F32),
        in_specs=[SMEM] + [VMEM] * 15,
        out_specs=VMEM,
        scratch_shapes=[pltpu.VMEM((128, 1536), F32), pltpu.VMEM((192, 128), F32)],
        compiler_params=params(16),
        cost_estimate=pl.CostEstimate(flops=10**9, bytes_accessed=3 * 10**6, transcendentals=0),
        name="elementals",
    )(directions, *kets, *waves, phase, turn)


def phases_kernel(momenta, directions, phase, turn):
    site = lax.broadcasted_iota(jnp.int32, (4, L * L), 1)
    z_at = lax.axis_index("space").astype(jnp.int32) * 4 + lax.broadcasted_iota(jnp.int32, (4, L * L), 0)
    for mom in range(2):
        product = momenta[mom, 0] * (site & 15) + momenta[mom, 1] * (site >> 4) + momenta[mom, 2] * z_at
        angles = 2.0 * math.pi / L * (product & 15).astype(F32)
        phase[2 * mom] = jnp.cos(angles)
        phase[2 * mom + 1] = jnp.sin(angles)
    lane = lax.broadcasted_iota(jnp.int32, (8, 128), 1)
    for pair in range(3):
        axis = directions[pair]
        step = jnp.where(lane < 64, momenta[0, axis], momenta[1, axis])
        angles = 2.0 * math.pi / L * (step & 15).astype(F32)
        turn[0, pair] = jnp.cos(angles)
        turn[1, pair] = jnp.where(lane % 64 < 32, -jnp.sin(angles), jnp.sin(angles))


def phases(momenta, directions):
    return pl.pallas_call(
        phases_kernel,
        out_shape=(
            jax.ShapeDtypeStruct((4, 4, 256), F32),
            jax.ShapeDtypeStruct((2, 3, 8, 128), F32),
        ),
        in_specs=[SMEM] * 2,
        out_specs=(VMEM,) * 2,
        compiler_params=params(4),
        name="phases",
    )(momenta, directions)


def prepare_kernel(ins_time, sink_time, source, sink, far_hi, far_lo, near_hi, near_lo, own_hi, own_lo,
                   sink_hi, sink_lo, turned):
    tins = lax.axis_index("tins").astype(jnp.int32)
    weight = jnp.where(ins_time[0] < sink_time[0], 1.0, 0.0)
    slots = (
        (2, far_hi, far_lo, 0),
        (1, near_hi, near_lo, 0),
        (3, near_hi, near_lo, 256),
        (0, own_hi, own_lo, 0),
    )
    for part in range(2):
        for spin in range(NSPIN):
            rows = [
                source[part, spin * 128 + i * 32 + j * 8 : spin * 128 + i * 32 + j * 8 + 8, :]
                for j in range(4)
                for i in range(4)
            ]
            turned[...] = jnp.concatenate(rows, axis=0).T
            sign = 1 if part == 0 else -1
            same = slice(part * 512 + spin * 128, part * 512 + spin * 128 + 128)
            other = slice((1 - part) * 512 + spin * 128, (1 - part) * 512 + spin * 128 + 128)
            for offset, to_hi, to_lo, top in slots:
                block = pl.multiple_of(((tins + offset) & 3) * 128, 128)
                high, low = halves(turned[pl.ds(block, 128), :])
                to_hi[top : top + 128, same] = sign * high
                to_lo[top : top + 128, same] = sign * low
                to_hi[top + 128 : top + 256, other] = high
                to_lo[top + 128 : top + 256, other] = low
    for part in range(2):
        for spin in range(NSPIN):
            sign = 1.0 if spin < 2 else -1.0
            value = sink[part, :, spin * 128 : spin * 128 + 128].T * (sign * weight)
            high, low = halves(value)
            sink_hi[part * 128 : part * 128 + 128, spin * 128 : spin * 128 + 128] = high
            sink_lo[part * 128 : part * 128 + 128, spin * 128 : spin * 128 + 128] = low


def prepare(ins_time, sink_time, source, sink):
    one = jax.ShapeDtypeStruct((256, 1024), BF16)
    two = jax.ShapeDtypeStruct((512, 1024), BF16)
    snk = jax.ShapeDtypeStruct((256, 512), BF16)
    return pl.pallas_call(
        prepare_kernel,
        out_shape=(one, one, two, two, one, one, snk, snk),
        in_specs=[SMEM] * 2 + [VMEM] * 2,
        out_specs=(VMEM,) * 8,
        scratch_shapes=[pltpu.VMEM((512, 128), F32)],
        compiler_params=params(12),
        cost_estimate=pl.CostEstimate(flops=10**8, bytes_accessed=8 * 10**6, transcendentals=0),
        name="prepare",
    )(ins_time, sink_time, source, sink)


def left_kernel(mine, others, sink_hi, sink_lo, src_hi, src_lo, left_hi, left_lo, out_re, out_im):
    core, z_hi, x_at = lax.axis_index("space") & 1, z_place(), x_place()
    for pair in range(3):
        rows_all = []
        for x_pos in range(4):
            from_x = (x_at - x_pos) & 3
            tiles = []
            for i in range(4):
                from_z = (z_hi - i) & 3
                for group in range(2):
                    own = mine[from_x, from_z, group, pair]
                    other = others[from_x, from_z, group, pair]
                    tiles.append(jnp.where(core == 0, own, other))
                    tiles.append(jnp.where(core == 0, other, own))
            turned = jnp.concatenate(tiles, axis=0).T
            swapped = jnp.concatenate(
                [-turned[32:64], turned[0:32], -turned[96:128], turned[64:96]], axis=0
            )
            rows_all.append(jnp.concatenate([turned, swapped], axis=1))
        value = dot_three(
            halves(jnp.concatenate(rows_all, axis=0)), (sink_hi[...], sink_lo[...]), ((1,), (0,))
        )
        high, low = halves(value)
        for x_pos in range(4):
            for mom in range(2):
                for part in range(2):
                    start = x_pos * 128 + mom * 64 + part * 32
                    for spin in range(NSPIN):
                        at = part * 512 + spin * 128 + x_pos * 32
                        lanes = slice((mom * 3 + pair) * 128, (mom * 3 + pair) * 128 + 128)
                        cols = slice(spin * 128, spin * 128 + 128)
                        left_hi[at : at + 32, lanes] = high[start : start + 32, cols]
                        left_lo[at : at + 32, lanes] = low[start : start + 32, cols]
    right_kernel(src_hi, src_lo, left_hi, left_lo, out_re, out_im)


def left_product(mine, others, sink_hi, sink_lo, src_hi, src_lo):
    shape = jax.ShapeDtypeStruct((1024, 768), BF16)
    result = jax.ShapeDtypeStruct((128, 768), F32)
    return pl.pallas_call(
        left_kernel,
        out_shape=(shape, shape, result, result),
        in_specs=[VMEM] * 6,
        out_specs=(VMEM,) * 4,
        compiler_params=params(16),
        cost_estimate=pl.CostEstimate(flops=10**9, bytes_accessed=4 * 10**6, transcendentals=0),
        name="left",
    )(mine, others, sink_hi, sink_lo, src_hi, src_lo)


def right_kernel(src_hi, src_lo, left_hi, left_lo, *outs):
    for block in range(len(outs) // 2):
        rows = slice(block * 256, block * 256 + 256)
        value = dot_three(
            (src_hi[rows, :], src_lo[rows, :]), (left_hi[...], left_lo[...]), ((1,), (0,))
        )
        outs[2 * block][...] = value[0:128]
        outs[2 * block + 1][...] = value[128:256]


def right_product(src_hi, src_lo, left_hi, left_lo):
    count = 2 * (src_hi.shape[0] // 256)
    return pl.pallas_call(
        right_kernel,
        out_shape=(jax.ShapeDtypeStruct((128, 768), F32),) * count,
        in_specs=[VMEM] * 4,
        out_specs=(VMEM,) * count,
        compiler_params=params(16),
        cost_estimate=pl.CostEstimate(flops=10**9, bytes_accessed=5 * 10**6, transcendentals=0),
        name="right",
    )(src_hi, src_lo, left_hi, left_lo)


def relay_kernel(first, second, third, fourth, out_one, out_two):
    out_one[...] = first[...] + second[...]
    out_two[...] = third[...] + fourth[...]


def relay_sums(*terms):
    shape = jax.ShapeDtypeStruct((128, 768), F32)
    return pl.pallas_call(
        relay_kernel,
        out_shape=(shape, shape),
        in_specs=[VMEM] * 4,
        out_specs=(VMEM,) * 2,
        compiler_params=params(8),
        name="relay",
    )(*terms)


def final_kernel(*refs):
    out = refs[6]
    for part in range(2):
        value = refs[part][...] + (refs[2 + part][...] + refs[4 + part][...])
        for pair in range(6):
            out[:, pair, part, :] = value[:, pair * 128 : pair * 128 + 128]


def final_sum(*terms):
    return pl.pallas_call(
        final_kernel,
        out_shape=jax.ShapeDtypeStruct((128, 6, 2, 128), F32),
        in_specs=[VMEM] * 6,
        out_specs=VMEM,
        compiler_params=params(8),
        name="final",
    )(*terms)


def ring(count, step):
    return [(i, (i + step) % count) for i in range(count)]


def along_x(step):
    return [(i * 4 + j, i * 4 + (j + step) % 4) for i in range(4) for j in range(4)]


def along_z(step):
    return [(i * 4 + j, ((i + step) % 4) * 4 + j) for i in range(4) for j in range(4)]


def neighbours(block, along):
    return lax.ppermute(block, "tsink", along(1)), lax.ppermute(block, "tsink", along(-1))


def opposite(behind, ahead, along):
    return lax.ppermute(behind[0], "tsink", along(1)), lax.ppermute(ahead[1], "tsink", along(-1))


def on_device(eigvecs, links, momenta, directions, ins_time, sink_time, sink_peramb, source_peramb):
    depth = eigvecs.shape[4]
    links = links[0].reshape(54, depth, 256)
    own = packed(eigvecs[0])
    below = lax.ppermute(own[:, depth - 1 :], "space", ring(4, 1))
    above = lax.ppermute(own[:, :1], "space", ring(4, -1))
    ket_near = neighbours(own, along_z)
    bra = jnp.concatenate([below, own, above], axis=1)
    bra_near = neighbours(bra, along_x)
    top = lax.ppermute(links[36:, depth - 1], "space", ring(4, 1))

    phase, turn = phases(momenta, directions)
    waves_own = wave_blocks(1, [bra], links, top)
    ket_near, phase = lax.optimization_barrier((ket_near, phase))
    bra_near, waves_own = lax.optimization_barrier((bra_near, waves_own))
    ket_far = opposite(*ket_near, along_z)
    bra_far = opposite(*bra_near, along_x)

    waves_near = wave_blocks(2, bra_near, links, top)
    waves_far = wave_blocks(1, bra_far, links, top)
    waves = (*waves_own, *waves_near[:2], *waves_far, *waves_near[2:])
    kets = (own, ket_near[0], *ket_far, ket_near[1])
    blocks = elemental_blocks(directions, kets, waves, phase, turn)
    core_pairs = [(i, i ^ 1) for i in range(4)]
    summed = (
        blocks[0]
        + lax.ppermute(blocks[1], "space", core_pairs)
        + lax.ppermute(blocks[0], "space", [(i, i ^ 2) for i in range(4)])
        + lax.ppermute(blocks[1], "space", [(i, i ^ 3) for i in range(4)])
    )
    sources = prepare(ins_time, sink_time, source_peramb[0], sink_peramb[0, 0])
    columns = [lax.ppermute(summed, "tsink", along_z(d)) for d in (1, 2, 3)]
    columns, sources = lax.optimization_barrier((columns, sources))
    far_hi, far_lo, near_hi, near_lo, own_hi, own_lo, sink_hi, sink_lo = sources
    summed = jnp.stack([summed] + list(columns))
    summed = jnp.stack([summed] + [lax.ppermute(summed, "tsink", along_x(d)) for d in (1, 2, 3)])
    others = lax.ppermute(summed, "space", core_pairs)

    left_hi, left_lo, far_re, far_im = left_product(
        summed, others, sink_hi, sink_lo, far_hi, far_lo
    )

    def up(value):
        return lax.ppermute(value, "tins", ring(4, 1))

    def down(value):
        return lax.ppermute(value, "tins", ring(4, -1))

    from_below, from_above = up(far_re), down(far_im)
    next_re, next_im, prev_re, prev_im = right_product(near_hi, near_lo, left_hi, left_lo)
    own_re, own_im = right_product(own_hi, own_lo, left_hi, left_lo)
    next_im, prev_re, own_re, own_im = lax.optimization_barrier((next_im, prev_re, own_re, own_im))
    below_im, above_re = up(next_im), down(prev_re)
    next_re, prev_im = relay_sums(next_re, from_below, prev_im, from_above)
    below_re, above_im = up(next_re), down(prev_im)
    return final_sum(own_re, own_im, below_re, below_im, above_re, above_im)[:, None]


def solution(mesh):
    in_specs = (
        P("tins", None, None, "tsink", "space", None),
        P("tins", None, None, None, None, "space", None),
        P(),
        P(),
        P("tins"),
        P("tsink"),
        P("tsink", "tins", None, "space", None),
        P("tins", None, None, None),
    )
    out_specs = P("tins", "tsink", None, None, "space")
    return jax.shard_map(
        on_device, mesh=mesh, in_specs=in_specs, out_specs=out_specs, check_vma=False
    )
```

```python
import functools
import math

import jax
import jax.numpy as jnp
from jax import lax
from jax.experimental import pallas as pl
from jax.experimental.pallas import tpu as pltpu
from jax.sharding import PartitionSpec as P

L = 16
NSPIN = 4
F32 = jnp.float32
BF16 = jnp.bfloat16
VMEM = pl.BlockSpec(memory_space=pltpu.VMEM)
SMEM = pl.BlockSpec(memory_space=pltpu.SMEM)


def params(mib):
    return pltpu.CompilerParams(vmem_limit_bytes=mib * 2**20)


def halves(value):
    high = value.astype(BF16)
    return high, (value - high.astype(F32)).astype(BF16)


def dot_three(first, second, dims):
    dot = functools.partial(
        lax.dot_general, dimension_numbers=(dims, ((), ())), preferred_element_type=F32
    )
    return dot(first[0], second[0]) + (dot(first[0], second[1]) + dot(first[1], second[0]))


def colour_product(link, vector, adjoint):
    out = []
    for colour in range(3):
        real = imag = None
        for inner in range(3):
            v_re, v_im = vector[inner], vector[3 + inner]
            if adjoint:
                u_re, u_im = link(inner, colour)
                terms = (u_re * v_re + u_im * v_im, u_re * v_im - u_im * v_re)
            else:
                u_re, u_im = link(colour, inner)
                terms = (u_re * v_re - u_im * v_im, u_re * v_im + u_im * v_re)
            real = terms[0] if real is None else real + terms[0]
            imag = terms[1] if imag is None else imag + terms[1]
        out.append((real, imag))
    return [pair[0] for pair in out] + [pair[1] for pair in out]


def shift_x(value, step, column):
    if step == 1:
        return jnp.where(
            column == L - 1, pltpu.roll(value, L - 1, 1), pltpu.roll(value, 127, 1)
        )
    return jnp.where(column == 0, pltpu.roll(value, 128 - L + 1, 1), pltpu.roll(value, 1, 1))


def shift_y(low, high, step, lane):
    if step == 1:
        low, high = pltpu.roll(low, 128 - L, 1), pltpu.roll(high, 128 - L, 1)
        own = lane < 128 - L
    else:
        low, high = pltpu.roll(low, L, 1), pltpu.roll(high, L, 1)
        own = lane >= L
    return jnp.where(own, low, high), jnp.where(own, high, low)


def z_place():
    return lax.shift_right_logical(lax.axis_index("tsink").astype(jnp.int32), 2)


def x_place():
    return lax.axis_index("tsink").astype(jnp.int32) & 3


def block_readers(refs):
    def whole(ref):
        return lambda z, comp, lanes: ref[comp // 3, z, comp % 3, :, lanes]

    def pair(real, imag):
        return lambda z, comp, lanes: (real, imag)[comp // 3][z, comp % 3, :, lanes]

    readers, at = [], 0
    while at < len(refs):
        if len(refs[at].shape) == 5:
            readers.append(whole(refs[at]))
            at += 1
        else:
            readers.append(pair(refs[at], refs[at + 1]))
            at += 2
    return readers


def pack_kernel(eig_far, own, eig, sem):
    copy = pltpu.make_async_copy(eig_far, eig, sem)
    copy.start()
    copy.wait()
    for part in range(2):
        for colour in range(3):
            for z in range(4):
                own[part, z, colour] = eig[part, colour, :, z, :]


def packed(eig):
    return pl.pallas_call(
        pack_kernel,
        out_shape=jax.ShapeDtypeStruct((2, 4, 3, 8, 256), F32),
        in_specs=[pl.BlockSpec(memory_space=pltpu.HBM)],
        out_specs=VMEM,
        scratch_shapes=[pltpu.VMEM((2, 3, 8, 4, 256), F32), pltpu.SemaphoreType.DMA],
        compiler_params=params(8),
        name="pack",
    )(eig)


def waves_kernel(count, *refs):
    blocks = block_readers(refs[: len(refs) - 2 - 2 * count])
    links, low_links = refs[len(refs) - 2 - 2 * count : len(refs) - 2 * count]
    outs = refs[len(refs) - 2 * count :]
    lane = lax.broadcasted_iota(jnp.int32, (8, 128), 1)
    column = lane % L
    for z in range(4):
        for block, read in enumerate(blocks):
            high, low = outs[2 * block], outs[2 * block + 1]

            def vec(z_at, half):
                lanes = slice(half * 128, half * 128 + 128)
                return [read(z_at, comp, lanes) for comp in range(6)]

            here = [vec(z + 1, half) for half in range(2)]
            for axis in range(3):

                def link(half, shifted):
                    lanes = slice(half * 128, half * 128 + 128)

                    def row(index):
                        if not shifted:
                            return links[axis * 18 + index, z : z + 1, lanes]
                        if z == 0:
                            return low_links[index : index + 1, lanes]
                        return links[axis * 18 + index, z - 1 : z, lanes]

                    return lambda a, b: (row(a * 3 + b), row(9 + a * 3 + b))

                use = [link(half, False) for half in range(2)]
                below = [link(half, axis == 2) for half in range(2)]
                if axis == 0:
                    above = [[shift_x(v, 1, column) for v in here[h]] for h in range(2)]
                elif axis == 1:
                    pairs = [shift_y(a, b, 1, lane) for a, b in zip(here[0], here[1])]
                    above = [[pair[h] for pair in pairs] for h in range(2)]
                else:
                    above = [vec(z + 2, half) for half in range(2)]
                ahead = [colour_product(use[h], above[h], False) for h in range(2)]
                source = here if axis < 2 else [vec(z, half) for half in range(2)]
                back = [colour_product(below[h], source[h], True) for h in range(2)]
                if axis == 0:
                    back = [[shift_x(v, -1, column) for v in back[h]] for h in range(2)]
                elif axis == 1:
                    pairs = [shift_y(a, b, -1, lane) for a, b in zip(back[0], back[1])]
                    back = [[pair[h] for pair in pairs] for h in range(2)]
                for half in range(2):
                    for comp in range(6):
                        cols = slice(comp * 256 + half * 128, comp * 256 + half * 128 + 128)
                        both = jnp.concatenate([ahead[half][comp], back[half][comp]], axis=0)
                        parts = halves(both)
                        high[z, axis * 16 : axis * 16 + 16, cols] = parts[0]
                        low[z, axis * 16 : axis * 16 + 16, cols] = parts[1]


def wave_blocks(count, blocks, links, low_links):
    shape = jax.ShapeDtypeStruct((4, 48, 1536), BF16)
    return pl.pallas_call(
        functools.partial(waves_kernel, count),
        out_shape=(shape,) * (2 * count),
        in_specs=[VMEM] * (len(blocks) + 2),
        out_specs=(VMEM,) * (2 * count),
        compiler_params=params(8),
        cost_estimate=pl.CostEstimate(
            flops=count * 10**7, bytes_accessed=count * 2 * 10**6, transcendentals=0
        ),
        name="waves",
    )(*blocks, links, low_links)


def elemental_kernel(directions, *refs):
    kets = block_readers(refs[0:5])
    waves = refs[5:13]
    phase, turn, out, phased, total = refs[13:]
    core, z_hi, x_at = lax.axis_index("space").astype(jnp.int32) & 1, z_place(), x_place()
    for z in range(4):
        for block in range(4):
            row = pl.multiple_of(((z_hi - block) & 3) * 8, 8)
            ket = kets[block]
            for mom in range(2):
                cos = phase[mom * 2, z : z + 1, :]
                sin = phase[mom * 2 + 1, z : z + 1, :]
                for colour in range(3):
                    v_re, v_im = ket(z, colour, slice(0, 256)), ket(z, 3 + colour, slice(0, 256))
                    w_re = cos * v_re + sin * v_im
                    w_im = cos * v_im - sin * v_re
                    first = slice(colour * 256, colour * 256 + 256)
                    second = slice(768 + colour * 256, 1024 + colour * 256)
                    phased[pl.ds(mom * 64 + row, 8), first] = w_re
                    phased[pl.ds(mom * 64 + row, 8), second] = w_im
                    phased[pl.ds(mom * 64 + 32 + row, 8), first] = w_im
                    phased[pl.ds(mom * 64 + 32 + row, 8), second] = -w_re
        bras = jnp.concatenate(
            [waves[2 * block + part][z] for part in range(2) for block in range(4)], axis=0
        )
        value = lax.dot_general(
            bras,
            jnp.concatenate(halves(phased[...]), axis=0),
            (((1,), (1,)), ((), ())),
            preferred_element_type=F32,
        )
        value = value[:192] + value[192:]
        value = value[:, :128] + value[:, 128:]
        total[...] = value if z == 0 else total[...] + value

    is_real = lax.broadcasted_iota(jnp.int32, (8, 128), 1) % 64 < 32
    for pair in range(3):
        axis = directions[pair]
        for block in range(4):
            row = pl.multiple_of(block * 48 + axis * 16, 16)
            ahead, back = total[pl.ds(row, 8), :], total[pl.ds(row + 8, 8), :]
            added = ahead + back
            swapped = jnp.where(is_real, pltpu.roll(added, 96, 1), pltpu.roll(added, 32, 1))
            group = (x_at - block) & 3
            out[core ^ (group & 1), lax.shift_right_logical(group, 1), pair] = (
                turn[0, pair] * (back - ahead) + turn[1, pair] * swapped
            )


def elemental_blocks(directions, kets, waves, phase, turn):
    return pl.pallas_call(
        elemental_kernel,
        out_shape=jax.ShapeDtypeStruct((2, 2, 3, 8, 128), F32),
        in_specs=[SMEM] + [VMEM] * 15,
        out_specs=VMEM,
        scratch_shapes=[pltpu.VMEM((128, 1536), F32), pltpu.VMEM((192, 128), F32)],
        compiler_params=params(16),
        cost_estimate=pl.CostEstimate(flops=10**9, bytes_accessed=3 * 10**6, transcendentals=0),
        name="elementals",
    )(directions, *kets, *waves, phase, turn)


def phases_kernel(momenta, directions, phase, turn):
    site = lax.broadcasted_iota(jnp.int32, (4, L * L), 1)
    z_at = lax.axis_index("space").astype(jnp.int32) * 4 + lax.broadcasted_iota(jnp.int32, (4, L * L), 0)
    for mom in range(2):
        product = momenta[mom, 0] * (site & 15) + momenta[mom, 1] * (site >> 4) + momenta[mom, 2] * z_at
        angles = 2.0 * math.pi / L * (product & 15).astype(F32)
        phase[2 * mom] = jnp.cos(angles)
        phase[2 * mom + 1] = jnp.sin(angles)
    lane = lax.broadcasted_iota(jnp.int32, (8, 128), 1)
    for pair in range(3):
        axis = directions[pair]
        step = jnp.where(lane < 64, momenta[0, axis], momenta[1, axis])
        angles = 2.0 * math.pi / L * (step & 15).astype(F32)
        turn[0, pair] = jnp.cos(angles)
        turn[1, pair] = jnp.where(lane % 64 < 32, -jnp.sin(angles), jnp.sin(angles))


def phases(momenta, directions):
    return pl.pallas_call(
        phases_kernel,
        out_shape=(
            jax.ShapeDtypeStruct((4, 4, 256), F32),
            jax.ShapeDtypeStruct((2, 3, 8, 128), F32),
        ),
        in_specs=[SMEM] * 2,
        out_specs=(VMEM,) * 2,
        compiler_params=params(4),
        name="phases",
    )(momenta, directions)


def prepare_kernel(ins_time, sink_time, source, sink, far_hi, far_lo, near_hi, near_lo, own_hi, own_lo,
                   sink_hi, sink_lo, turned):
    tins = lax.axis_index("tins").astype(jnp.int32)
    weight = jnp.where(ins_time[0] < sink_time[0], 1.0, 0.0)
    slots = (
        (2, far_hi, far_lo, 0),
        (1, near_hi, near_lo, 0),
        (3, near_hi, near_lo, 256),
        (0, own_hi, own_lo, 0),
    )
    for part in range(2):
        for spin in range(NSPIN):
            rows = [
                source[part, spin * 128 + i * 32 + j * 8 : spin * 128 + i * 32 + j * 8 + 8, :]
                for j in range(4)
                for i in range(4)
            ]
            turned[...] = jnp.concatenate(rows, axis=0).T
            sign = 1 if part == 0 else -1
            same = slice(part * 512 + spin * 128, part * 512 + spin * 128 + 128)
            other = slice((1 - part) * 512 + spin * 128, (1 - part) * 512 + spin * 128 + 128)
            for offset, to_hi, to_lo, top in slots:
                block = pl.multiple_of(((tins + offset) & 3) * 128, 128)
                high, low = halves(turned[pl.ds(block, 128), :])
                to_hi[top : top + 128, same] = sign * high
                to_lo[top : top + 128, same] = sign * low
                to_hi[top + 128 : top + 256, other] = high
                to_lo[top + 128 : top + 256, other] = low
    for part in range(2):
        for spin in range(NSPIN):
            sign = 1.0 if spin < 2 else -1.0
            value = sink[part, :, spin * 128 : spin * 128 + 128].T * (sign * weight)
            high, low = halves(value)
            sink_hi[part * 128 : part * 128 + 128, spin * 128 : spin * 128 + 128] = high
            sink_lo[part * 128 : part * 128 + 128, spin * 128 : spin * 128 + 128] = low


def prepare(ins_time, sink_time, source, sink):
    one = jax.ShapeDtypeStruct((256, 1024), BF16)
    two = jax.ShapeDtypeStruct((512, 1024), BF16)
    snk = jax.ShapeDtypeStruct((256, 512), BF16)
    return pl.pallas_call(
        prepare_kernel,
        out_shape=(one, one, two, two, one, one, snk, snk),
        in_specs=[SMEM] * 2 + [VMEM] * 2,
        out_specs=(VMEM,) * 8,
        scratch_shapes=[pltpu.VMEM((512, 128), F32)],
        compiler_params=params(12),
        cost_estimate=pl.CostEstimate(flops=10**8, bytes_accessed=8 * 10**6, transcendentals=0),
        name="prepare",
    )(ins_time, sink_time, source, sink)


def left_kernel(mine, others, sink_hi, sink_lo, src_hi, src_lo, left_hi, left_lo, out_re, out_im):
    core, z_hi, x_at = lax.axis_index("space") & 1, z_place(), x_place()
    for pair in range(3):
        rows_all = []
        for x_pos in range(4):
            from_x = (x_at - x_pos) & 3
            tiles = []
            for i in range(4):
                from_z = (z_hi - i) & 3
                for group in range(2):
                    own = mine[from_x, from_z, group, pair]
                    other = others[from_x, from_z, group, pair]
                    tiles.append(jnp.where(core == 0, own, other))
                    tiles.append(jnp.where(core == 0, other, own))
            turned = jnp.concatenate(tiles, axis=0).T
            swapped = jnp.concatenate(
                [-turned[32:64], turned[0:32], -turned[96:128], turned[64:96]], axis=0
            )
            rows_all.append(jnp.concatenate([turned, swapped], axis=1))
        value = dot_three(
            halves(jnp.concatenate(rows_all, axis=0)), (sink_hi[...], sink_lo[...]), ((1,), (0,))
        )
        high, low = halves(value)
        for x_pos in range(4):
            for mom in range(2):
                for part in range(2):
                    start = x_pos * 128 + mom * 64 + part * 32
                    for spin in range(NSPIN):
                        at = part * 512 + spin * 128 + x_pos * 32
                        lanes = slice((mom * 3 + pair) * 128, (mom * 3 + pair) * 128 + 128)
                        cols = slice(spin * 128, spin * 128 + 128)
                        left_hi[at : at + 32, lanes] = high[start : start + 32, cols]
                        left_lo[at : at + 32, lanes] = low[start : start + 32, cols]
    right_kernel(src_hi, src_lo, left_hi, left_lo, out_re, out_im)


def left_product(mine, others, sink_hi, sink_lo, src_hi, src_lo):
    shape = jax.ShapeDtypeStruct((1024, 768), BF16)
    result = jax.ShapeDtypeStruct((128, 768), F32)
    return pl.pallas_call(
        left_kernel,
        out_shape=(shape, shape, result, result),
        in_specs=[VMEM] * 6,
        out_specs=(VMEM,) * 4,
        compiler_params=params(16),
        cost_estimate=pl.CostEstimate(flops=10**9, bytes_accessed=4 * 10**6, transcendentals=0),
        name="left",
    )(mine, others, sink_hi, sink_lo, src_hi, src_lo)


def right_kernel(src_hi, src_lo, left_hi, left_lo, *outs):
    for block in range(len(outs) // 2):
        rows = slice(block * 256, block * 256 + 256)
        value = dot_three(
            (src_hi[rows, :], src_lo[rows, :]), (left_hi[...], left_lo[...]), ((1,), (0,))
        )
        outs[2 * block][...] = value[0:128]
        outs[2 * block + 1][...] = value[128:256]


def right_product(src_hi, src_lo, left_hi, left_lo):
    count = 2 * (src_hi.shape[0] // 256)
    return pl.pallas_call(
        right_kernel,
        out_shape=(jax.ShapeDtypeStruct((128, 768), F32),) * count,
        in_specs=[VMEM] * 4,
        out_specs=(VMEM,) * count,
        compiler_params=params(16),
        cost_estimate=pl.CostEstimate(flops=10**9, bytes_accessed=5 * 10**6, transcendentals=0),
        name="right",
    )(src_hi, src_lo, left_hi, left_lo)


def relay_kernel(first, second, third, fourth, out_one, out_two):
    out_one[...] = first[...] + second[...]
    out_two[...] = third[...] + fourth[...]


def relay_sums(*terms):
    shape = jax.ShapeDtypeStruct((128, 768), F32)
    return pl.pallas_call(
        relay_kernel,
        out_shape=(shape, shape),
        in_specs=[VMEM] * 4,
        out_specs=(VMEM,) * 2,
        compiler_params=params(8),
        name="relay",
    )(*terms)


def final_kernel(*refs):
    out = refs[6]
    for part in range(2):
        value = refs[part][...] + (refs[2 + part][...] + refs[4 + part][...])
        for pair in range(6):
            out[:, pair, part, :] = value[:, pair * 128 : pair * 128 + 128]


def final_sum(*terms):
    return pl.pallas_call(
        final_kernel,
        out_shape=jax.ShapeDtypeStruct((128, 6, 2, 128), F32),
        in_specs=[VMEM] * 6,
        out_specs=VMEM,
        compiler_params=params(8),
        name="final",
    )(*terms)


def ring(count, step):
    return [(i, (i + step) % count) for i in range(count)]


def along_x(step):
    return [(i * 4 + j, i * 4 + (j + step) % 4) for i in range(4) for j in range(4)]


def along_z(step):
    return [(i * 4 + j, ((i + step) % 4) * 4 + j) for i in range(4) for j in range(4)]


def neighbours(block, along):
    return lax.ppermute(block, "tsink", along(1)), lax.ppermute(block, "tsink", along(-1))


def opposite(behind, ahead, along):
    return lax.ppermute(behind[0], "tsink", along(1)), lax.ppermute(ahead[1], "tsink", along(-1))


def on_device(eigvecs, links, momenta, directions, ins_time, sink_time, sink_peramb, source_peramb):
    depth = eigvecs.shape[4]
    links = links[0].reshape(54, depth, 256)
    own = packed(eigvecs[0])
    below = lax.ppermute(own[:, depth - 1 :], "space", ring(4, 1))
    above = lax.ppermute(own[:, :1], "space", ring(4, -1))
    ket_near = neighbours(own, along_z)
    bra = jnp.concatenate([below, own, above], axis=1)
    bra_near = neighbours(bra, along_x)
    top = lax.ppermute(links[36:, depth - 1], "space", ring(4, 1))

    phase, turn = phases(momenta, directions)
    waves_own = wave_blocks(1, [bra], links, top)
    ket_far = opposite(*ket_near, along_z)
    ket_near, waves_own, phase = lax.optimization_barrier((ket_near, waves_own, phase))
    waves_near = wave_blocks(2, bra_near, links, top)
    bra_near, waves_near = lax.optimization_barrier((bra_near, waves_near))
    bra_far = opposite(*bra_near, along_x)

    waves_far = wave_blocks(1, bra_far, links, top)
    waves = (*waves_own, *waves_near[:2], *waves_far, *waves_near[2:])
    kets = (own, ket_near[0], *ket_far, ket_near[1])
    blocks = elemental_blocks(directions, kets, waves, phase, turn)
    core_pairs = [(i, i ^ 1) for i in range(4)]
    summed = (
        blocks[0]
        + lax.ppermute(blocks[1], "space", core_pairs)
        + lax.ppermute(blocks[0], "space", [(i, i ^ 2) for i in range(4)])
        + lax.ppermute(blocks[1], "space", [(i, i ^ 3) for i in range(4)])
    )
    sources = prepare(ins_time, sink_time, source_peramb[0], sink_peramb[0, 0])
    columns = [lax.ppermute(summed, "tsink", along_z(d)) for d in (1, 2, 3)]
    columns, sources = lax.optimization_barrier((columns, sources))
    far_hi, far_lo, near_hi, near_lo, own_hi, own_lo, sink_hi, sink_lo = sources
    summed = jnp.stack([summed] + list(columns))
    summed = jnp.stack([summed] + [lax.ppermute(summed, "tsink", along_x(d)) for d in (1, 2, 3)])
    others = lax.ppermute(summed, "space", core_pairs)

    left_hi, left_lo, far_re, far_im = left_product(
        summed, others, sink_hi, sink_lo, far_hi, far_lo
    )

    def up(value):
        return lax.ppermute(value, "tins", ring(4, 1))

    def down(value):
        return lax.ppermute(value, "tins", ring(4, -1))

    from_below, from_above = up(far_re), down(far_im)
    next_re, next_im, prev_re, prev_im = right_product(near_hi, near_lo, left_hi, left_lo)
    own_re, own_im = right_product(own_hi, own_lo, left_hi, left_lo)
    next_im, prev_re, own_re, own_im = lax.optimization_barrier((next_im, prev_re, own_re, own_im))
    below_im, above_re = up(next_im), down(prev_re)
    next_re, prev_im = relay_sums(next_re, from_below, prev_im, from_above)
    below_re, above_im = up(next_re), down(prev_im)
    return final_sum(own_re, own_im, below_re, below_im, above_re, above_im)[:, None]


def solution(mesh):
    in_specs = (
        P("tins", None, None, "tsink", "space", None),
        P("tins", None, None, None, None, "space", None),
        P(),
        P(),
        P("tins"),
        P("tsink"),
        P("tsink", "tins", None, "space", None),
        P("tins", None, None, None),
    )
    out_specs = P("tins", "tsink", None, None, "space")
    return jax.shard_map(
        on_device, mesh=mesh, in_specs=in_specs, out_specs=out_specs, check_vma=False
    )
```

```python
import functools
import math

import jax
import jax.numpy as jnp
from jax import lax
from jax.experimental import pallas as pl
from jax.experimental.pallas import tpu as pltpu
from jax.sharding import PartitionSpec as P

L = 16
NSPIN = 4
F32 = jnp.float32
BF16 = jnp.bfloat16
VMEM = pl.BlockSpec(memory_space=pltpu.VMEM)
SMEM = pl.BlockSpec(memory_space=pltpu.SMEM)


def params(mib):
    return pltpu.CompilerParams(vmem_limit_bytes=mib * 2**20)


def halves(value):
    high = value.astype(BF16)
    return high, (value - high.astype(F32)).astype(BF16)


def dot_three(first, second, dims):
    dot = functools.partial(
        lax.dot_general, dimension_numbers=(dims, ((), ())), preferred_element_type=F32
    )
    return dot(first[0], second[0]) + (dot(first[0], second[1]) + dot(first[1], second[0]))


def colour_product(link, vector, adjoint):
    out = []
    for colour in range(3):
        real = imag = None
        for inner in range(3):
            v_re, v_im = vector[inner], vector[3 + inner]
            if adjoint:
                u_re, u_im = link(inner, colour)
                terms = (u_re * v_re + u_im * v_im, u_re * v_im - u_im * v_re)
            else:
                u_re, u_im = link(colour, inner)
                terms = (u_re * v_re - u_im * v_im, u_re * v_im + u_im * v_re)
            real = terms[0] if real is None else real + terms[0]
            imag = terms[1] if imag is None else imag + terms[1]
        out.append((real, imag))
    return [pair[0] for pair in out] + [pair[1] for pair in out]


def shift_x(value, step, column):
    if step == 1:
        return jnp.where(
            column == L - 1, pltpu.roll(value, L - 1, 1), pltpu.roll(value, 127, 1)
        )
    return jnp.where(column == 0, pltpu.roll(value, 128 - L + 1, 1), pltpu.roll(value, 1, 1))


def shift_y(low, high, step, lane):
    if step == 1:
        low, high = pltpu.roll(low, 128 - L, 1), pltpu.roll(high, 128 - L, 1)
        own = lane < 128 - L
    else:
        low, high = pltpu.roll(low, L, 1), pltpu.roll(high, L, 1)
        own = lane >= L
    return jnp.where(own, low, high), jnp.where(own, high, low)


def z_place():
    return lax.shift_right_logical(lax.axis_index("tsink").astype(jnp.int32), 2)


def x_place():
    return lax.axis_index("tsink").astype(jnp.int32) & 3


def block_readers(refs):
    def whole(ref):
        return lambda z, comp, lanes: ref[comp // 3, z, comp % 3, :, lanes]

    def pair(real, imag):
        return lambda z, comp, lanes: (real, imag)[comp // 3][z, comp % 3, :, lanes]

    readers, at = [], 0
    while at < len(refs):
        if len(refs[at].shape) == 5:
            readers.append(whole(refs[at]))
            at += 1
        else:
            readers.append(pair(refs[at], refs[at + 1]))
            at += 2
    return readers


def pack_kernel(eig_far, own, eig, sem):
    copy = pltpu.make_async_copy(eig_far, eig, sem)
    copy.start()
    copy.wait()
    for part in range(2):
        for colour in range(3):
            for z in range(4):
                own[part, z, colour] = eig[part, colour, :, z, :]


def packed(eig):
    return pl.pallas_call(
        pack_kernel,
        out_shape=jax.ShapeDtypeStruct((2, 4, 3, 8, 256), F32),
        in_specs=[pl.BlockSpec(memory_space=pltpu.HBM)],
        out_specs=VMEM,
        scratch_shapes=[pltpu.VMEM((2, 3, 8, 4, 256), F32), pltpu.SemaphoreType.DMA],
        compiler_params=params(8),
        name="pack",
    )(eig)


def waves_kernel(count, *refs):
    blocks = block_readers(refs[: len(refs) - 2 - 2 * count])
    links, low_links = refs[len(refs) - 2 - 2 * count : len(refs) - 2 * count]
    outs = refs[len(refs) - 2 * count :]
    lane = lax.broadcasted_iota(jnp.int32, (8, 128), 1)
    column = lane % L
    for z in range(4):
        for block, read in enumerate(blocks):
            high, low = outs[2 * block], outs[2 * block + 1]

            def vec(z_at, half):
                lanes = slice(half * 128, half * 128 + 128)
                return [read(z_at, comp, lanes) for comp in range(6)]

            here = [vec(z + 1, half) for half in range(2)]
            for axis in range(3):

                def link(half, shifted):
                    lanes = slice(half * 128, half * 128 + 128)

                    def row(index):
                        if not shifted:
                            return links[axis * 18 + index, z : z + 1, lanes]
                        if z == 0:
                            return low_links[index : index + 1, lanes]
                        return links[axis * 18 + index, z - 1 : z, lanes]

                    return lambda a, b: (row(a * 3 + b), row(9 + a * 3 + b))

                use = [link(half, False) for half in range(2)]
                below = [link(half, axis == 2) for half in range(2)]
                if axis == 0:
                    above = [[shift_x(v, 1, column) for v in here[h]] for h in range(2)]
                elif axis == 1:
                    pairs = [shift_y(a, b, 1, lane) for a, b in zip(here[0], here[1])]
                    above = [[pair[h] for pair in pairs] for h in range(2)]
                else:
                    above = [vec(z + 2, half) for half in range(2)]
                ahead = [colour_product(use[h], above[h], False) for h in range(2)]
                source = here if axis < 2 else [vec(z, half) for half in range(2)]
                back = [colour_product(below[h], source[h], True) for h in range(2)]
                if axis == 0:
                    back = [[shift_x(v, -1, column) for v in back[h]] for h in range(2)]
                elif axis == 1:
                    pairs = [shift_y(a, b, -1, lane) for a, b in zip(back[0], back[1])]
                    back = [[pair[h] for pair in pairs] for h in range(2)]
                for half in range(2):
                    for comp in range(6):
                        cols = slice(comp * 256 + half * 128, comp * 256 + half * 128 + 128)
                        both = jnp.concatenate([ahead[half][comp], back[half][comp]], axis=0)
                        parts = halves(both)
                        high[z, axis * 16 : axis * 16 + 16, cols] = parts[0]
                        low[z, axis * 16 : axis * 16 + 16, cols] = parts[1]


def wave_blocks(count, blocks, links, low_links):
    shape = jax.ShapeDtypeStruct((4, 48, 1536), BF16)
    return pl.pallas_call(
        functools.partial(waves_kernel, count),
        out_shape=(shape,) * (2 * count),
        in_specs=[VMEM] * (len(blocks) + 2),
        out_specs=(VMEM,) * (2 * count),
        compiler_params=params(8),
        cost_estimate=pl.CostEstimate(
            flops=count * 10**7, bytes_accessed=count * 2 * 10**6, transcendentals=0
        ),
        name="waves",
    )(*blocks, links, low_links)


def elemental_kernel(directions, *refs):
    kets = block_readers(refs[0:5])
    waves = refs[5:13]
    phase, turn, out, phased, total = refs[13:]
    core, z_hi, x_at = lax.axis_index("space").astype(jnp.int32) & 1, z_place(), x_place()
    for z in range(4):
        for block in range(4):
            row = pl.multiple_of(((z_hi - block) & 3) * 8, 8)
            ket = kets[block]
            for mom in range(2):
                cos = phase[mom * 2, z : z + 1, :]
                sin = phase[mom * 2 + 1, z : z + 1, :]
                for colour in range(3):
                    v_re, v_im = ket(z, colour, slice(0, 256)), ket(z, 3 + colour, slice(0, 256))
                    w_re = cos * v_re + sin * v_im
                    w_im = cos * v_im - sin * v_re
                    first = slice(colour * 256, colour * 256 + 256)
                    second = slice(768 + colour * 256, 1024 + colour * 256)
                    phased[pl.ds(mom * 64 + row, 8), first] = w_re
                    phased[pl.ds(mom * 64 + row, 8), second] = w_im
                    phased[pl.ds(mom * 64 + 32 + row, 8), first] = w_im
                    phased[pl.ds(mom * 64 + 32 + row, 8), second] = -w_re
        bras = jnp.concatenate(
            [waves[2 * block + part][z] for part in range(2) for block in range(4)], axis=0
        )
        value = lax.dot_general(
            bras,
            jnp.concatenate(halves(phased[...]), axis=0),
            (((1,), (1,)), ((), ())),
            preferred_element_type=F32,
        )
        value = value[:192] + value[192:]
        value = value[:, :128] + value[:, 128:]
        total[...] = value if z == 0 else total[...] + value

    is_real = lax.broadcasted_iota(jnp.int32, (8, 128), 1) % 64 < 32
    for pair in range(3):
        axis = directions[pair]
        for block in range(4):
            row = pl.multiple_of(block * 48 + axis * 16, 16)
            ahead, back = total[pl.ds(row, 8), :], total[pl.ds(row + 8, 8), :]
            added = ahead + back
            swapped = jnp.where(is_real, pltpu.roll(added, 96, 1), pltpu.roll(added, 32, 1))
            group = (x_at - block) & 3
            out[core ^ (group & 1), lax.shift_right_logical(group, 1), pair] = (
                turn[0, pair] * (back - ahead) + turn[1, pair] * swapped
            )


def elemental_blocks(directions, kets, waves, phase, turn):
    return pl.pallas_call(
        elemental_kernel,
        out_shape=jax.ShapeDtypeStruct((2, 2, 3, 8, 128), F32),
        in_specs=[SMEM] + [VMEM] * 15,
        out_specs=VMEM,
        scratch_shapes=[pltpu.VMEM((128, 1536), F32), pltpu.VMEM((192, 128), F32)],
        compiler_params=params(16),
        cost_estimate=pl.CostEstimate(flops=10**9, bytes_accessed=3 * 10**6, transcendentals=0),
        name="elementals",
    )(directions, *kets, *waves, phase, turn)


def phases_kernel(momenta, directions, phase, turn):
    site = lax.broadcasted_iota(jnp.int32, (4, L * L), 1)
    z_at = lax.axis_index("space").astype(jnp.int32) * 4 + lax.broadcasted_iota(jnp.int32, (4, L * L), 0)
    for mom in range(2):
        product = momenta[mom, 0] * (site & 15) + momenta[mom, 1] * (site >> 4) + momenta[mom, 2] * z_at
        angles = 2.0 * math.pi / L * (product & 15).astype(F32)
        phase[2 * mom] = jnp.cos(angles)
        phase[2 * mom + 1] = jnp.sin(angles)
    lane = lax.broadcasted_iota(jnp.int32, (8, 128), 1)
    for pair in range(3):
        axis = directions[pair]
        step = jnp.where(lane < 64, momenta[0, axis], momenta[1, axis])
        angles = 2.0 * math.pi / L * (step & 15).astype(F32)
        turn[0, pair] = jnp.cos(angles)
        turn[1, pair] = jnp.where(lane % 64 < 32, -jnp.sin(angles), jnp.sin(angles))


def phases(momenta, directions):
    return pl.pallas_call(
        phases_kernel,
        out_shape=(
            jax.ShapeDtypeStruct((4, 4, 256), F32),
            jax.ShapeDtypeStruct((2, 3, 8, 128), F32),
        ),
        in_specs=[SMEM] * 2,
        out_specs=(VMEM,) * 2,
        compiler_params=params(4),
        name="phases",
    )(momenta, directions)


def prepare_kernel(ins_time, sink_time, source, sink, far_hi, far_lo, near_hi, near_lo, own_hi, own_lo,
                   sink_hi, sink_lo, turned):
    tins = lax.axis_index("tins").astype(jnp.int32)
    weight = jnp.where(ins_time[0] < sink_time[0], 1.0, 0.0)
    slots = (
        (2, far_hi, far_lo, 0),
        (1, near_hi, near_lo, 0),
        (3, near_hi, near_lo, 256),
        (0, own_hi, own_lo, 0),
    )
    for part in range(2):
        for spin in range(NSPIN):
            rows = [
                source[part, spin * 128 + i * 32 + j * 8 : spin * 128 + i * 32 + j * 8 + 8, :]
                for j in range(4)
                for i in range(4)
            ]
            turned[...] = jnp.concatenate(rows, axis=0).T
            sign = 1 if part == 0 else -1
            same = slice(part * 512 + spin * 128, part * 512 + spin * 128 + 128)
            other = slice((1 - part) * 512 + spin * 128, (1 - part) * 512 + spin * 128 + 128)
            for offset, to_hi, to_lo, top in slots:
                block = pl.multiple_of(((tins + offset) & 3) * 128, 128)
                high, low = halves(turned[pl.ds(block, 128), :])
                to_hi[top : top + 128, same] = sign * high
                to_lo[top : top + 128, same] = sign * low
                to_hi[top + 128 : top + 256, other] = high
                to_lo[top + 128 : top + 256, other] = low
    for part in range(2):
        for spin in range(NSPIN):
            sign = 1.0 if spin < 2 else -1.0
            value = sink[part, :, spin * 128 : spin * 128 + 128].T * (sign * weight)
            high, low = halves(value)
            sink_hi[part * 128 : part * 128 + 128, spin * 128 : spin * 128 + 128] = high
            sink_lo[part * 128 : part * 128 + 128, spin * 128 : spin * 128 + 128] = low


def prepare(ins_time, sink_time, source, sink):
    one = jax.ShapeDtypeStruct((256, 1024), BF16)
    two = jax.ShapeDtypeStruct((512, 1024), BF16)
    snk = jax.ShapeDtypeStruct((256, 512), BF16)
    return pl.pallas_call(
        prepare_kernel,
        out_shape=(one, one, two, two, one, one, snk, snk),
        in_specs=[SMEM] * 2 + [VMEM] * 2,
        out_specs=(VMEM,) * 8,
        scratch_shapes=[pltpu.VMEM((512, 128), F32)],
        compiler_params=params(12),
        cost_estimate=pl.CostEstimate(flops=10**8, bytes_accessed=8 * 10**6, transcendentals=0),
        name="prepare",
    )(ins_time, sink_time, source, sink)


def left_kernel(mine, others, sink_hi, sink_lo, src_hi, src_lo, left_hi, left_lo, out_re, out_im):
    core, z_hi, x_at = lax.axis_index("space") & 1, z_place(), x_place()
    for pair in range(3):
        rows_all = []
        for x_pos in range(4):
            from_x = (x_at - x_pos) & 3
            tiles = []
            for i in range(4):
                from_z = (z_hi - i) & 3
                for group in range(2):
                    own = mine[from_x, from_z, group, pair]
                    other = others[from_x, from_z, group, pair]
                    tiles.append(jnp.where(core == 0, own, other))
                    tiles.append(jnp.where(core == 0, other, own))
            turned = jnp.concatenate(tiles, axis=0).T
            swapped = jnp.concatenate(
                [-turned[32:64], turned[0:32], -turned[96:128], turned[64:96]], axis=0
            )
            rows_all.append(jnp.concatenate([turned, swapped], axis=1))
        value = dot_three(
            halves(jnp.concatenate(rows_all, axis=0)), (sink_hi[...], sink_lo[...]), ((1,), (0,))
        )
        high, low = halves(value)
        for x_pos in range(4):
            for mom in range(2):
                for part in range(2):
                    start = x_pos * 128 + mom * 64 + part * 32
                    for spin in range(NSPIN):
                        at = part * 512 + spin * 128 + x_pos * 32
                        lanes = slice((mom * 3 + pair) * 128, (mom * 3 + pair) * 128 + 128)
                        cols = slice(spin * 128, spin * 128 + 128)
                        left_hi[at : at + 32, lanes] = high[start : start + 32, cols]
                        left_lo[at : at + 32, lanes] = low[start : start + 32, cols]
    right_kernel(src_hi, src_lo, left_hi, left_lo, out_re, out_im)


def left_product(mine, others, sink_hi, sink_lo, src_hi, src_lo):
    shape = jax.ShapeDtypeStruct((1024, 768), BF16)
    result = jax.ShapeDtypeStruct((128, 768), F32)
    return pl.pallas_call(
        left_kernel,
        out_shape=(shape, shape, result, result),
        in_specs=[VMEM] * 6,
        out_specs=(VMEM,) * 4,
        compiler_params=params(16),
        cost_estimate=pl.CostEstimate(flops=10**9, bytes_accessed=4 * 10**6, transcendentals=0),
        name="left",
    )(mine, others, sink_hi, sink_lo, src_hi, src_lo)


def right_kernel(src_hi, src_lo, left_hi, left_lo, *outs):
    for block in range(len(outs) // 2):
        rows = slice(block * 256, block * 256 + 256)
        value = dot_three(
            (src_hi[rows, :], src_lo[rows, :]), (left_hi[...], left_lo[...]), ((1,), (0,))
        )
        outs[2 * block][...] = value[0:128]
        outs[2 * block + 1][...] = value[128:256]


def right_product(src_hi, src_lo, left_hi, left_lo):
    count = 2 * (src_hi.shape[0] // 256)
    return pl.pallas_call(
        right_kernel,
        out_shape=(jax.ShapeDtypeStruct((128, 768), F32),) * count,
        in_specs=[VMEM] * 4,
        out_specs=(VMEM,) * count,
        compiler_params=params(16),
        cost_estimate=pl.CostEstimate(flops=10**9, bytes_accessed=5 * 10**6, transcendentals=0),
        name="right",
    )(src_hi, src_lo, left_hi, left_lo)


def relay_kernel(first, second, third, fourth, out_one, out_two):
    out_one[...] = first[...] + second[...]
    out_two[...] = third[...] + fourth[...]


def relay_sums(*terms):
    shape = jax.ShapeDtypeStruct((128, 768), F32)
    return pl.pallas_call(
        relay_kernel,
        out_shape=(shape, shape),
        in_specs=[VMEM] * 4,
        out_specs=(VMEM,) * 2,
        compiler_params=params(8),
        name="relay",
    )(*terms)


def final_kernel(*refs):
    out = refs[6]
    for part in range(2):
        value = refs[part][...] + (refs[2 + part][...] + refs[4 + part][...])
        for pair in range(6):
            out[:, pair, part, :] = value[:, pair * 128 : pair * 128 + 128]


def final_sum(*terms):
    return pl.pallas_call(
        final_kernel,
        out_shape=jax.ShapeDtypeStruct((128, 6, 2, 128), F32),
        in_specs=[VMEM] * 6,
        out_specs=VMEM,
        compiler_params=params(8),
        name="final",
    )(*terms)


def ring(count, step):
    return [(i, (i + step) % count) for i in range(count)]


def along_x(step):
    return [(i * 4 + j, i * 4 + (j + step) % 4) for i in range(4) for j in range(4)]


def along_z(step):
    return [(i * 4 + j, ((i + step) % 4) * 4 + j) for i in range(4) for j in range(4)]


def neighbours(block, along):
    return lax.ppermute(block, "tsink", along(1)), lax.ppermute(block, "tsink", along(-1))


def opposite(behind, ahead, along):
    return lax.ppermute(behind[0], "tsink", along(1)), lax.ppermute(ahead[1], "tsink", along(-1))


def on_device(eigvecs, links, momenta, directions, ins_time, sink_time, sink_peramb, source_peramb):
    depth = eigvecs.shape[4]
    links = links[0].reshape(54, depth, 256)
    own = packed(eigvecs[0])
    below = lax.ppermute(own[:, depth - 1 :], "space", ring(4, 1))
    above = lax.ppermute(own[:, :1], "space", ring(4, -1))
    ket_near = neighbours(own, along_z)
    bra = jnp.concatenate([below, own, above], axis=1)
    bra_near = neighbours(bra, along_x)
    top = lax.ppermute(links[36:, depth - 1], "space", ring(4, 1))

    phase, turn = phases(momenta, directions)
    waves_own = wave_blocks(1, [bra], links, top)
    ket_near, waves_own = lax.optimization_barrier((ket_near, waves_own))
    bra_near, waves_own = lax.optimization_barrier((bra_near, waves_own))
    ket_far = opposite(*ket_near, along_z)
    bra_far = opposite(*bra_near, along_x)
    waves_near = wave_blocks(2, bra_near, links, top)
    waves_near, phase, turn = lax.optimization_barrier((waves_near, phase, turn))
    waves_far = wave_blocks(1, bra_far, links, top)
    waves = (*waves_own, *waves_near[:2], *waves_far, *waves_near[2:])
    kets = (own, ket_near[0], *ket_far, ket_near[1])
    blocks = elemental_blocks(directions, kets, waves, phase, turn)
    core_pairs = [(i, i ^ 1) for i in range(4)]
    summed = (
        blocks[0]
        + lax.ppermute(blocks[1], "space", core_pairs)
        + lax.ppermute(blocks[0], "space", [(i, i ^ 2) for i in range(4)])
        + lax.ppermute(blocks[1], "space", [(i, i ^ 3) for i in range(4)])
    )
    sources = prepare(ins_time, sink_time, source_peramb[0], sink_peramb[0, 0])
    columns = [lax.ppermute(summed, "tsink", along_z(d)) for d in (1, 2, 3)]
    columns, sources = lax.optimization_barrier((columns, sources))
    far_hi, far_lo, near_hi, near_lo, own_hi, own_lo, sink_hi, sink_lo = sources
    summed = jnp.stack([summed] + list(columns))
    summed = jnp.stack([summed] + [lax.ppermute(summed, "tsink", along_x(d)) for d in (1, 2, 3)])
    others = lax.ppermute(summed, "space", core_pairs)

    left_hi, left_lo, far_re, far_im = left_product(
        summed, others, sink_hi, sink_lo, far_hi, far_lo
    )

    def up(value):
        return lax.ppermute(value, "tins", ring(4, 1))

    def down(value):
        return lax.ppermute(value, "tins", ring(4, -1))

    from_below, from_above = up(far_re), down(far_im)
    next_re, next_im, prev_re, prev_im = right_product(near_hi, near_lo, left_hi, left_lo)
    own_re, own_im = right_product(own_hi, own_lo, left_hi, left_lo)
    next_im, prev_re, own_re, own_im = lax.optimization_barrier((next_im, prev_re, own_re, own_im))
    below_im, above_re = up(next_im), down(prev_re)
    next_re, prev_im = relay_sums(next_re, from_below, prev_im, from_above)
    below_re, above_im = up(next_re), down(prev_im)
    return final_sum(own_re, own_im, below_re, below_im, above_re, above_im)[:, None]


def solution(mesh):
    in_specs = (
        P("tins", None, None, "tsink", "space", None),
        P("tins", None, None, None, None, "space", None),
        P(),
        P(),
        P("tins"),
        P("tsink"),
        P("tsink", "tins", None, "space", None),
        P("tins", None, None, None),
    )
    out_specs = P("tins", "tsink", None, None, "space")
    return jax.shard_map(
        on_device, mesh=mesh, in_specs=in_specs, out_specs=out_specs, check_vma=False
    )
```

```python
import functools
import math

import jax
import jax.numpy as jnp
from jax import lax
from jax.experimental import pallas as pl
from jax.experimental.pallas import tpu as pltpu
from jax.sharding import PartitionSpec as P

L = 16
NSPIN = 4
F32 = jnp.float32
BF16 = jnp.bfloat16
VMEM = pl.BlockSpec(memory_space=pltpu.VMEM)
SMEM = pl.BlockSpec(memory_space=pltpu.SMEM)


def params(mib):
    return pltpu.CompilerParams(vmem_limit_bytes=mib * 2**20)


def halves(value):
    high = value.astype(BF16)
    return high, (value - high.astype(F32)).astype(BF16)


def dot_three(first, second, dims):
    dot = functools.partial(
        lax.dot_general, dimension_numbers=(dims, ((), ())), preferred_element_type=F32
    )
    return dot(first[0], second[0]) + (dot(first[0], second[1]) + dot(first[1], second[0]))


def colour_product(link, vector, adjoint):
    out = []
    for colour in range(3):
        real = imag = None
        for inner in range(3):
            v_re, v_im = vector[inner], vector[3 + inner]
            if adjoint:
                u_re, u_im = link(inner, colour)
                terms = (u_re * v_re + u_im * v_im, u_re * v_im - u_im * v_re)
            else:
                u_re, u_im = link(colour, inner)
                terms = (u_re * v_re - u_im * v_im, u_re * v_im + u_im * v_re)
            real = terms[0] if real is None else real + terms[0]
            imag = terms[1] if imag is None else imag + terms[1]
        out.append((real, imag))
    return [pair[0] for pair in out] + [pair[1] for pair in out]


def shift_x(value, step, column):
    if step == 1:
        return jnp.where(
            column == L - 1, pltpu.roll(value, L - 1, 1), pltpu.roll(value, 127, 1)
        )
    return jnp.where(column == 0, pltpu.roll(value, 128 - L + 1, 1), pltpu.roll(value, 1, 1))


def shift_y(low, high, step, lane):
    if step == 1:
        low, high = pltpu.roll(low, 128 - L, 1), pltpu.roll(high, 128 - L, 1)
        own = lane < 128 - L
    else:
        low, high = pltpu.roll(low, L, 1), pltpu.roll(high, L, 1)
        own = lane >= L
    return jnp.where(own, low, high), jnp.where(own, high, low)


def z_place():
    return lax.shift_right_logical(lax.axis_index("tsink").astype(jnp.int32), 2)


def x_place():
    return lax.axis_index("tsink").astype(jnp.int32) & 3


def block_readers(refs):
    def whole(ref):
        return lambda z, comp, lanes: ref[comp // 3, z, comp % 3, :, lanes]

    def pair(real, imag):
        return lambda z, comp, lanes: (real, imag)[comp // 3][z, comp % 3, :, lanes]

    readers, at = [], 0
    while at < len(refs):
        if len(refs[at].shape) == 5:
            readers.append(whole(refs[at]))
            at += 1
        else:
            readers.append(pair(refs[at], refs[at + 1]))
            at += 2
    return readers


def pack_kernel(eig_far, own, eig, sem):
    copy = pltpu.make_async_copy(eig_far, eig, sem)
    copy.start()
    copy.wait()
    for part in range(2):
        for colour in range(3):
            for z in range(4):
                own[part, z, colour] = eig[part, colour, :, z, :]


def packed(eig):
    return pl.pallas_call(
        pack_kernel,
        out_shape=jax.ShapeDtypeStruct((2, 4, 3, 8, 256), F32),
        in_specs=[pl.BlockSpec(memory_space=pltpu.HBM)],
        out_specs=VMEM,
        scratch_shapes=[pltpu.VMEM((2, 3, 8, 4, 256), F32), pltpu.SemaphoreType.DMA],
        compiler_params=params(8),
        name="pack",
    )(eig)


def waves_kernel(count, *refs):
    blocks = block_readers(refs[: len(refs) - 2 - 2 * count])
    links, low_links = refs[len(refs) - 2 - 2 * count : len(refs) - 2 * count]
    outs = refs[len(refs) - 2 * count :]
    lane = lax.broadcasted_iota(jnp.int32, (8, 128), 1)
    column = lane % L
    for z in range(4):
        for block, read in enumerate(blocks):
            high, low = outs[2 * block], outs[2 * block + 1]

            def vec(z_at, half):
                lanes = slice(half * 128, half * 128 + 128)
                return [read(z_at, comp, lanes) for comp in range(6)]

            here = [vec(z + 1, half) for half in range(2)]
            for axis in range(3):

                def link(half, shifted):
                    lanes = slice(half * 128, half * 128 + 128)

                    def row(index):
                        if not shifted:
                            return links[axis * 18 + index, z : z + 1, lanes]
                        if z == 0:
                            return low_links[index : index + 1, lanes]
                        return links[axis * 18 + index, z - 1 : z, lanes]

                    return lambda a, b: (row(a * 3 + b), row(9 + a * 3 + b))

                use = [link(half, False) for half in range(2)]
                below = [link(half, axis == 2) for half in range(2)]
                if axis == 0:
                    above = [[shift_x(v, 1, column) for v in here[h]] for h in range(2)]
                elif axis == 1:
                    pairs = [shift_y(a, b, 1, lane) for a, b in zip(here[0], here[1])]
                    above = [[pair[h] for pair in pairs] for h in range(2)]
                else:
                    above = [vec(z + 2, half) for half in range(2)]
                ahead = [colour_product(use[h], above[h], False) for h in range(2)]
                source = here if axis < 2 else [vec(z, half) for half in range(2)]
                back = [colour_product(below[h], source[h], True) for h in range(2)]
                if axis == 0:
                    back = [[shift_x(v, -1, column) for v in back[h]] for h in range(2)]
                elif axis == 1:
                    pairs = [shift_y(a, b, -1, lane) for a, b in zip(back[0], back[1])]
                    back = [[pair[h] for pair in pairs] for h in range(2)]
                for half in range(2):
                    for comp in range(6):
                        cols = slice(comp * 256 + half * 128, comp * 256 + half * 128 + 128)
                        both = jnp.concatenate([ahead[half][comp], back[half][comp]], axis=0)
                        parts = halves(both)
                        high[z, axis * 16 : axis * 16 + 16, cols] = parts[0]
                        low[z, axis * 16 : axis * 16 + 16, cols] = parts[1]


def wave_blocks(count, blocks, links, low_links):
    shape = jax.ShapeDtypeStruct((4, 48, 1536), BF16)
    return pl.pallas_call(
        functools.partial(waves_kernel, count),
        out_shape=(shape,) * (2 * count),
        in_specs=[VMEM] * (len(blocks) + 2),
        out_specs=(VMEM,) * (2 * count),
        compiler_params=params(8),
        cost_estimate=pl.CostEstimate(
            flops=count * 10**7, bytes_accessed=count * 2 * 10**6, transcendentals=0
        ),
        name="waves",
    )(*blocks, links, low_links)


def elemental_kernel(directions, *refs):
    kets = block_readers(refs[0:5])
    waves = refs[5:13]
    phase, turn, out, phased, total = refs[13:]
    core, z_hi, x_at = lax.axis_index("space").astype(jnp.int32) & 1, z_place(), x_place()
    for z in range(4):
        for block in range(4):
            row = pl.multiple_of(((z_hi - block) & 3) * 8, 8)
            ket = kets[block]
            for mom in range(2):
                cos = phase[mom * 2, z : z + 1, :]
                sin = phase[mom * 2 + 1, z : z + 1, :]
                for colour in range(3):
                    v_re, v_im = ket(z, colour, slice(0, 256)), ket(z, 3 + colour, slice(0, 256))
                    w_re = cos * v_re + sin * v_im
                    w_im = cos * v_im - sin * v_re
                    first = slice(colour * 256, colour * 256 + 256)
                    second = slice(768 + colour * 256, 1024 + colour * 256)
                    phased[pl.ds(mom * 64 + row, 8), first] = w_re
                    phased[pl.ds(mom * 64 + row, 8), second] = w_im
                    phased[pl.ds(mom * 64 + 32 + row, 8), first] = w_im
                    phased[pl.ds(mom * 64 + 32 + row, 8), second] = -w_re
        bras = jnp.concatenate(
            [waves[2 * block + part][z] for part in range(2) for block in range(4)], axis=0
        )
        value = lax.dot_general(
            bras,
            jnp.concatenate(halves(phased[...]), axis=0),
            (((1,), (1,)), ((), ())),
            preferred_element_type=F32,
        )
        value = value[:192] + value[192:]
        value = value[:, :128] + value[:, 128:]
        total[...] = value if z == 0 else total[...] + value

    is_real = lax.broadcasted_iota(jnp.int32, (8, 128), 1) % 64 < 32
    for pair in range(3):
        axis = directions[pair]
        for block in range(4):
            row = pl.multiple_of(block * 48 + axis * 16, 16)
            ahead, back = total[pl.ds(row, 8), :], total[pl.ds(row + 8, 8), :]
            added = ahead + back
            swapped = jnp.where(is_real, pltpu.roll(added, 96, 1), pltpu.roll(added, 32, 1))
            group = (x_at - block) & 3
            out[core ^ (group & 1), lax.shift_right_logical(group, 1), pair] = (
                turn[0, pair] * (back - ahead) + turn[1, pair] * swapped
            )


def elemental_blocks(directions, kets, waves, phase, turn):
    return pl.pallas_call(
        elemental_kernel,
        out_shape=jax.ShapeDtypeStruct((2, 2, 3, 8, 128), F32),
        in_specs=[SMEM] + [VMEM] * 15,
        out_specs=VMEM,
        scratch_shapes=[pltpu.VMEM((128, 1536), F32), pltpu.VMEM((192, 128), F32)],
        compiler_params=params(16),
        cost_estimate=pl.CostEstimate(flops=10**9, bytes_accessed=3 * 10**6, transcendentals=0),
        name="elementals",
    )(directions, *kets, *waves, phase, turn)


def phases_kernel(momenta, directions, phase, turn):
    site = lax.broadcasted_iota(jnp.int32, (4, L * L), 1)
    z_at = lax.axis_index("space").astype(jnp.int32) * 4 + lax.broadcasted_iota(jnp.int32, (4, L * L), 0)
    for mom in range(2):
        product = momenta[mom, 0] * (site & 15) + momenta[mom, 1] * (site >> 4) + momenta[mom, 2] * z_at
        angles = 2.0 * math.pi / L * (product & 15).astype(F32)
        phase[2 * mom] = jnp.cos(angles)
        phase[2 * mom + 1] = jnp.sin(angles)
    lane = lax.broadcasted_iota(jnp.int32, (8, 128), 1)
    for pair in range(3):
        axis = directions[pair]
        step = jnp.where(lane < 64, momenta[0, axis], momenta[1, axis])
        angles = 2.0 * math.pi / L * (step & 15).astype(F32)
        turn[0, pair] = jnp.cos(angles)
        turn[1, pair] = jnp.where(lane % 64 < 32, -jnp.sin(angles), jnp.sin(angles))


def phases(momenta, directions):
    return pl.pallas_call(
        phases_kernel,
        out_shape=(
            jax.ShapeDtypeStruct((4, 4, 256), F32),
            jax.ShapeDtypeStruct((2, 3, 8, 128), F32),
        ),
        in_specs=[SMEM] * 2,
        out_specs=(VMEM,) * 2,
        compiler_params=params(4),
        name="phases",
    )(momenta, directions)


def prepare_kernel(ins_time, sink_time, source, sink, far_hi, far_lo, near_hi, near_lo, own_hi, own_lo,
                   sink_hi, sink_lo, turned):
    tins = lax.axis_index("tins").astype(jnp.int32)
    weight = jnp.where(ins_time[0] < sink_time[0], 1.0, 0.0)
    slots = (
        (2, far_hi, far_lo, 0),
        (1, near_hi, near_lo, 0),
        (3, near_hi, near_lo, 256),
        (0, own_hi, own_lo, 0),
    )
    for part in range(2):
        for spin in range(NSPIN):
            rows = [
                source[part, spin * 128 + i * 32 + j * 8 : spin * 128 + i * 32 + j * 8 + 8, :]
                for j in range(4)
                for i in range(4)
            ]
            turned[...] = jnp.concatenate(rows, axis=0).T
            sign = 1 if part == 0 else -1
            same = slice(part * 512 + spin * 128, part * 512 + spin * 128 + 128)
            other = slice((1 - part) * 512 + spin * 128, (1 - part) * 512 + spin * 128 + 128)
            for offset, to_hi, to_lo, top in slots:
                block = pl.multiple_of(((tins + offset) & 3) * 128, 128)
                high, low = halves(turned[pl.ds(block, 128), :])
                to_hi[top : top + 128, same] = sign * high
                to_lo[top : top + 128, same] = sign * low
                to_hi[top + 128 : top + 256, other] = high
                to_lo[top + 128 : top + 256, other] = low
    for part in range(2):
        for spin in range(NSPIN):
            sign = 1.0 if spin < 2 else -1.0
            value = sink[part, :, spin * 128 : spin * 128 + 128].T * (sign * weight)
            high, low = halves(value)
            sink_hi[part * 128 : part * 128 + 128, spin * 128 : spin * 128 + 128] = high
            sink_lo[part * 128 : part * 128 + 128, spin * 128 : spin * 128 + 128] = low


def prepare(ins_time, sink_time, source, sink):
    one = jax.ShapeDtypeStruct((256, 1024), BF16)
    two = jax.ShapeDtypeStruct((512, 1024), BF16)
    snk = jax.ShapeDtypeStruct((256, 512), BF16)
    return pl.pallas_call(
        prepare_kernel,
        out_shape=(one, one, two, two, one, one, snk, snk),
        in_specs=[SMEM] * 2 + [VMEM] * 2,
        out_specs=(VMEM,) * 8,
        scratch_shapes=[pltpu.VMEM((512, 128), F32)],
        compiler_params=params(12),
        cost_estimate=pl.CostEstimate(flops=10**8, bytes_accessed=8 * 10**6, transcendentals=0),
        name="prepare",
    )(ins_time, sink_time, source, sink)


def left_kernel(mine, others, sink_hi, sink_lo, src_hi, src_lo, left_hi, left_lo, out_re, out_im):
    core, z_hi, x_at = lax.axis_index("space") & 1, z_place(), x_place()
    for pair in range(3):
        rows_all = []
        for x_pos in range(4):
            from_x = (x_at - x_pos) & 3
            tiles = []
            for i in range(4):
                from_z = (z_hi - i) & 3
                for group in range(2):
                    own = mine[from_x, from_z, group, pair]
                    other = others[from_x, from_z, group, pair]
                    tiles.append(jnp.where(core == 0, own, other))
                    tiles.append(jnp.where(core == 0, other, own))
            turned = jnp.concatenate(tiles, axis=0).T
            swapped = jnp.concatenate(
                [-turned[32:64], turned[0:32], -turned[96:128], turned[64:96]], axis=0
            )
            rows_all.append(jnp.concatenate([turned, swapped], axis=1))
        value = dot_three(
            halves(jnp.concatenate(rows_all, axis=0)), (sink_hi[...], sink_lo[...]), ((1,), (0,))
        )
        high, low = halves(value)
        for x_pos in range(4):
            for mom in range(2):
                for part in range(2):
                    start = x_pos * 128 + mom * 64 + part * 32
                    for spin in range(NSPIN):
                        at = part * 512 + spin * 128 + x_pos * 32
                        lanes = slice((mom * 3 + pair) * 128, (mom * 3 + pair) * 128 + 128)
                        cols = slice(spin * 128, spin * 128 + 128)
                        left_hi[at : at + 32, lanes] = high[start : start + 32, cols]
                        left_lo[at : at + 32, lanes] = low[start : start + 32, cols]
    right_kernel(src_hi, src_lo, left_hi, left_lo, out_re, out_im)


def left_product(mine, others, sink_hi, sink_lo, src_hi, src_lo):
    shape = jax.ShapeDtypeStruct((1024, 768), BF16)
    result = jax.ShapeDtypeStruct((128, 768), F32)
    return pl.pallas_call(
        left_kernel,
        out_shape=(shape, shape, result, result),
        in_specs=[VMEM] * 6,
        out_specs=(VMEM,) * 4,
        compiler_params=params(16),
        cost_estimate=pl.CostEstimate(flops=10**9, bytes_accessed=4 * 10**6, transcendentals=0),
        name="left",
    )(mine, others, sink_hi, sink_lo, src_hi, src_lo)


def right_kernel(src_hi, src_lo, left_hi, left_lo, *outs):
    for block in range(len(outs) // 2):
        rows = slice(block * 256, block * 256 + 256)
        value = dot_three(
            (src_hi[rows, :], src_lo[rows, :]), (left_hi[...], left_lo[...]), ((1,), (0,))
        )
        outs[2 * block][...] = value[0:128]
        outs[2 * block + 1][...] = value[128:256]


def right_product(src_hi, src_lo, left_hi, left_lo):
    count = 2 * (src_hi.shape[0] // 256)
    return pl.pallas_call(
        right_kernel,
        out_shape=(jax.ShapeDtypeStruct((128, 768), F32),) * count,
        in_specs=[VMEM] * 4,
        out_specs=(VMEM,) * count,
        compiler_params=params(16),
        cost_estimate=pl.CostEstimate(flops=10**9, bytes_accessed=5 * 10**6, transcendentals=0),
        name="right",
    )(src_hi, src_lo, left_hi, left_lo)


def relay_kernel(first, second, out):
    out[...] = first[...] + second[...]


def relay_sum(*terms):
    shape = jax.ShapeDtypeStruct((128, 768), F32)
    return pl.pallas_call(
        relay_kernel,
        out_shape=shape,
        in_specs=[VMEM] * 2,
        out_specs=VMEM,
        compiler_params=params(8),
        name="relay",
    )(*terms)


def final_kernel(*refs):
    out = refs[6]
    for part in range(2):
        value = refs[part][...] + (refs[2 + part][...] + refs[4 + part][...])
        for pair in range(6):
            out[:, pair, part, :] = value[:, pair * 128 : pair * 128 + 128]


def final_sum(*terms):
    return pl.pallas_call(
        final_kernel,
        out_shape=jax.ShapeDtypeStruct((128, 6, 2, 128), F32),
        in_specs=[VMEM] * 6,
        out_specs=VMEM,
        compiler_params=params(8),
        name="final",
    )(*terms)


def ring(count, step):
    return [(i, (i + step) % count) for i in range(count)]


def along_x(step):
    return [(i * 4 + j, i * 4 + (j + step) % 4) for i in range(4) for j in range(4)]


def along_z(step):
    return [(i * 4 + j, ((i + step) % 4) * 4 + j) for i in range(4) for j in range(4)]


def neighbours(block, along):
    return lax.ppermute(block, "tsink", along(1)), lax.ppermute(block, "tsink", along(-1))


def opposite(behind, ahead, along):
    return lax.ppermute(behind[0], "tsink", along(1)), lax.ppermute(ahead[1], "tsink", along(-1))


def on_device(eigvecs, links, momenta, directions, ins_time, sink_time, sink_peramb, source_peramb):
    depth = eigvecs.shape[4]
    links = links[0].reshape(54, depth, 256)
    own = packed(eigvecs[0])
    below = lax.ppermute(own[:, depth - 1 :], "space", ring(4, 1))
    above = lax.ppermute(own[:, :1], "space", ring(4, -1))
    ket_near = neighbours(own, along_z)
    bra = jnp.concatenate([below, own, above], axis=1)
    bra_near = neighbours(bra, along_x)
    top = lax.ppermute(links[36:, depth - 1], "space", ring(4, 1))

    phase, turn = phases(momenta, directions)
    waves_own = wave_blocks(1, [bra], links, top)
    ket_near, waves_own = lax.optimization_barrier((ket_near, waves_own))
    bra_near, waves_own = lax.optimization_barrier((bra_near, waves_own))
    ket_far = opposite(*ket_near, along_z)
    bra_far = opposite(*bra_near, along_x)
    waves_near = wave_blocks(2, bra_near, links, top)
    waves_near, phase, turn = lax.optimization_barrier((waves_near, phase, turn))
    waves_far = wave_blocks(1, bra_far, links, top)
    waves = (*waves_own, *waves_near[:2], *waves_far, *waves_near[2:])
    kets = (own, ket_near[0], *ket_far, ket_near[1])
    blocks = elemental_blocks(directions, kets, waves, phase, turn)
    core_pairs = [(i, i ^ 1) for i in range(4)]
    summed = (
        blocks[0]
        + lax.ppermute(blocks[1], "space", core_pairs)
        + lax.ppermute(blocks[0], "space", [(i, i ^ 2) for i in range(4)])
        + lax.ppermute(blocks[1], "space", [(i, i ^ 3) for i in range(4)])
    )
    sources = prepare(ins_time, sink_time, source_peramb[0], sink_peramb[0, 0])
    columns = [lax.ppermute(summed, "tsink", along_z(d)) for d in (1, 2, 3)]
    columns, sources = lax.optimization_barrier((columns, sources))
    far_hi, far_lo, near_hi, near_lo, own_hi, own_lo, sink_hi, sink_lo = sources
    summed = jnp.stack([summed] + list(columns))
    summed = jnp.stack([summed] + [lax.ppermute(summed, "tsink", along_x(d)) for d in (1, 2, 3)])
    others = lax.ppermute(summed, "space", core_pairs)

    left_hi, left_lo, far_re, far_im = left_product(
        summed, others, sink_hi, sink_lo, far_hi, far_lo
    )

    def up(value):
        return lax.ppermute(value, "tins", ring(4, 1))

    def down(value):
        return lax.ppermute(value, "tins", ring(4, -1))

    from_below, from_above = up(far_re), down(far_im)
    next_re, next_im, prev_re, prev_im = right_product(near_hi, near_lo, left_hi, left_lo)
    own_re, own_im = right_product(own_hi, own_lo, left_hi, left_lo)
    next_im, prev_re, own_re, own_im = lax.optimization_barrier((next_im, prev_re, own_re, own_im))
    below_im, above_re = up(next_im), down(prev_re)
    below_re = up(relay_sum(next_re, from_below))
    above_im = down(relay_sum(prev_im, from_above))
    return final_sum(own_re, own_im, below_re, below_im, above_re, above_im)[:, None]


def solution(mesh):
    in_specs = (
        P("tins", None, None, "tsink", "space", None),
        P("tins", None, None, None, None, "space", None),
        P(),
        P(),
        P("tins"),
        P("tsink"),
        P("tsink", "tins", None, "space", None),
        P("tins", None, None, None),
    )
    out_specs = P("tins", "tsink", None, None, "space")
    return jax.shard_map(
        on_device, mesh=mesh, in_specs=in_specs, out_specs=out_specs, check_vma=False
    )
```
